256 devices in a mesh: prompt: 8 (over x, y_hi), group: 16 (over z, y_lo), tensor: 2 (over core).
Axes of the slice: x: 4, y: 4 (y_hi: 2, y_lo: 2; y = y_hi * 2 + y_lo), z: 8, core: 2. Of those that a mesh axis runs over, the one named last changes fastest.
Arguments:
- queries: bfloat16 [8, 16, 256, 8, 8, 128], P('prompt', 'group', None, 'tensor'), may hold values from -6 to 6
- resp_keys: bfloat16 [8, 16, 256, 8, 128], P('prompt', 'group', None, 'tensor'), may hold values from -6 to 6
- resp_values: bfloat16 [8, 16, 256, 8, 128], P('prompt', 'group', None, 'tensor'), may hold values from -6 to 6
- prompt_keys: bfloat16 [8, 768, 8, 128], P('prompt', ('group', 'tensor')), may hold values from -6 to 6
- prompt_values: bfloat16 [8, 768, 8, 128], P('prompt', ('group', 'tensor')), may hold values from -6 to 6
- attn_out: bfloat16 [8, 16, 256, 8, 8, 128], P('prompt', 'group', None, 'tensor'), may hold values from -6 to 6
- grad_out: bfloat16 [8, 16, 256, 8, 8, 128], P('prompt', 'group', None, 'tensor'), may hold values from -1536 to 1536
- log_sums: float32 [8, 16, 8, 8, 256], P('prompt', 'group', 'tensor'), may hold values from 6.9 to 7.9
- prompt_lengths: int32 [8], P('prompt'), may hold values from 384 to 768
- resp_lengths: int32 [8, 16], P('prompt', 'group'), may hold values from 1 to 256
- rewards: int32 [8, 16], P('prompt', 'group'), may hold values from 0 to 896
- task_ids: int32 [8], P('prompt'), may hold values from 0 to 7
- task_weights: float32 [8], replicated, may hold values from 0.5 to 2
Outputs:
- grad_queries: bfloat16 [8, 16, 256, 8, 8, 128], P('prompt', 'group', None, 'tensor')
- grad_resp_keys: bfloat16 [8, 16, 256, 8, 128], P('prompt', 'group', None, 'tensor')
- grad_resp_values: bfloat16 [8, 16, 256, 8, 128], P('prompt', 'group', None, 'tensor')
- grad_prompt_keys: bfloat16 [8, 768, 8, 128], P('prompt', ('group', 'tensor'))
- grad_prompt_values: bfloat16 [8, 768, 8, 128], P('prompt', ('group', 'tensor'))
The draws below stay inside these ranges and needn't reach their ends.
All inputs are finite; a program needn't handle non-finite values.
Results may differ from the reference program's by a relative error of at most 0.034.
Values may be sent and summed in bfloat16 or wider, within the bound.
No kernel may reach another device: no remote copies, remote signals or barrier semaphores. Data moves between devices by JAX's collectives and lax.ppermute only.
A program may use at most 64 MiB of HBM per device.

```python
import math
import jax
import jax.numpy as jnp
from jax import lax

KVH = 8
QPK = 8
HD = 128
PLEN = 768
RMAX = 256
NTASK = 8
PROMPTS = 8
GROUP = 16


def plant(values, rng, least, high):
    longest = values.shape.index(max(values.shape))
    spots = []
    for shift in (0, 1):
        where = [jax.random.randint(jax.random.fold_in(rng, axis), (), 0, length) for axis, length in enumerate(values.shape)]
        where[longest] = (where[longest] + shift) % values.shape[longest]
        spots.append(tuple(where))
    return values.at[spots[0]].set(least).at[spots[1]].set(high)


def level_of(stream_key, extent, pieces, low, high):
    factor_of, own = 1.0, jax.random.fold_in(stream_key, 6)
    for axis_at, blocks in pieces:
        steps = jnp.exp(jax.random.uniform(jax.random.fold_in(own, axis_at), (blocks,), jnp.float32, low / len(pieces), high / len(pieces)))
        factor_of = factor_of * jnp.repeat(steps, extent[axis_at] // blocks).reshape([-1 if axis == axis_at else 1 for axis in range(len(extent))])
    return factor_of


def normal_values(rng, dims, scale, reach, pieces=(), held_as=jnp.bfloat16):
    drawn = jax.random.normal(rng, dims, jnp.float32) * scale
    if len(pieces) > 0:
        drawn = level_of(rng, dims, pieces, -0.22, 0.18) * drawn
    return jnp.clip(drawn, min=-reach, max=reach).astype(held_as)


def setup_inputs(seed: int = 0) -> dict:
    splits = jax.random.split(jax.random.key(seed), 14)
    return {
        "queries": normal_values(splits[0], (PROMPTS, GROUP, RMAX, KVH, QPK, HD), 1.0, 6.0, ((0, 8), (1, 16), (3, 2))),
        "resp_keys": normal_values(splits[1], (PROMPTS, GROUP, RMAX, KVH, HD), 1.0, 6.0, ((0, 8), (1, 16), (3, 2))),
        "resp_values": normal_values(splits[2], (PROMPTS, GROUP, RMAX, KVH, HD), 1.0, 6.0, ((0, 8), (1, 16), (3, 2))),
        "prompt_keys": normal_values(splits[3], (PROMPTS, PLEN, KVH, HD), 1.0, 6.0, ((0, 8), (1, 32))),
        "prompt_values": normal_values(splits[4], (PROMPTS, PLEN, KVH, HD), 1.0, 6.0, ((0, 8), (1, 32))),
        "attn_out": normal_values(splits[5], (PROMPTS, GROUP, RMAX, KVH, QPK, HD), 1.0, 6.0, ((0, 8), (1, 16), (3, 2))),
        "grad_out": normal_values(splits[6], (PROMPTS, GROUP, RMAX, KVH, QPK, HD), RMAX, 1536.0, ((0, 8), (1, 16), (3, 2))),
        "log_sums": jnp.clip(6.9 + 1.0 * jax.random.uniform(splits[7], (PROMPTS, GROUP, KVH, QPK, RMAX), jnp.float32) ** level_of(splits[7], (PROMPTS, GROUP, KVH, QPK, RMAX), ((0, 8), (1, 16), (2, 2)), -0.2, 0.2), 6.9, 7.9),
        "prompt_lengths": plant(jax.random.randint(splits[8], (PROMPTS,), PLEN // 2, PLEN + 1), jax.random.fold_in(splits[8], 1), PLEN // 2, PLEN).astype(jnp.int32),
        "resp_lengths": plant(jax.random.randint(splits[9], (PROMPTS, GROUP), 1, RMAX + 1), jax.random.fold_in(splits[9], 1), 1, RMAX).astype(jnp.int32),
        "rewards": plant(jax.random.randint(splits[10], (PROMPTS, GROUP), 0, 897), jax.random.fold_in(splits[10], 1), 0, 896).astype(jnp.int32),
        "task_ids": plant(jax.random.randint(splits[11], (PROMPTS,), 0, NTASK), jax.random.fold_in(splits[11], 1), 0, NTASK - 1).astype(jnp.int32),
        "task_weights": jnp.clip(jnp.exp(jax.random.uniform(splits[12], (NTASK,), jnp.float32, math.log(0.5), math.log(2.0))), 0.5, 2.0),
    }


def pick(array, index, axis):
    return lax.dynamic_index_in_dim(array, index, axis, keepdims=False)

def head_grads(q_head, do_head, delta_head, lse_head, keys, values, prompt_live):
    rows, per, width = q_head.shape
    total = keys.shape[0]
    prompt_slots = total - rows
    scale = width ** (-0.5)
    q_flat = q_head.reshape(rows * per, width)
    do_flat = do_head.reshape(rows * per, width)
    scores = jnp.dot(q_flat, keys.T, preferred_element_type=jnp.float32) * scale
    position = (jnp.arange(rows * per) // per)[:, None]
    column = jnp.arange(total)[None, :]
    visible = jnp.where(column < prompt_slots, column < prompt_live, column - prompt_slots <= position)
    lse_rows = lse_head.T.reshape(rows * per)[:, None]
    probs = jnp.where(visible, jnp.exp(scores - lse_rows), 0.0)
    dprobs = jnp.dot(do_flat, values.T, preferred_element_type=jnp.float32)
    dscores = probs * (dprobs - delta_head.reshape(rows * per)[:, None])
    probs_b = probs.astype(jnp.bfloat16)
    dscores_b = dscores.astype(jnp.bfloat16)
    grad_v = jnp.dot(probs_b.T, do_flat, preferred_element_type=jnp.float32)
    grad_k = jnp.dot(dscores_b.T, q_flat, preferred_element_type=jnp.float32) * scale
    grad_q = (jnp.dot(dscores_b, keys, preferred_element_type=jnp.float32) * scale).astype(jnp.bfloat16)
    return (grad_q.reshape(rows, per, width), grad_k, grad_v)

def response_grads(q_all, rk_all, rv_all, pk_all, pv_all, out_all, go_all, lse_all, prompt_live, length, coef):
    rows = q_all.shape[0]
    live = (jnp.arange(rows) < length)[:, None, None, None]
    scaled = jnp.where(live, coef * go_all.astype(jnp.float32), 0.0).astype(jnp.bfloat16)
    delta = lax.optimization_barrier(jnp.sum(scaled.astype(jnp.float32) * out_all.astype(jnp.float32), axis=-1))

    def per_head(head):
        keys = jnp.concatenate([pick(pk_all, head, 1), pick(rk_all, head, 1)], axis=0)
        values = jnp.concatenate([pick(pv_all, head, 1), pick(rv_all, head, 1)], axis=0)
        return head_grads(pick(q_all, head, 1), pick(scaled, head, 1), pick(delta, head, 1), pick(lse_all, head, 0), keys, values, prompt_live)
    grad_q, grad_k, grad_v = lax.map(per_head, jnp.arange(q_all.shape[1]))
    grad_q = jnp.transpose(grad_q, (1, 0, 2, 3))
    grad_k = jnp.transpose(grad_k, (1, 0, 2))
    grad_v = jnp.transpose(grad_v, (1, 0, 2))
    slots = pk_all.shape[0]
    return (grad_q, grad_k[:slots], grad_v[:slots], grad_k[slots:], grad_v[slots:])

def reference(queries, resp_keys, resp_values, prompt_keys, prompt_values, attn_out, grad_out, log_sums, prompt_lengths, resp_lengths, rewards, task_ids, task_weights):
    score = rewards.astype(jnp.float32) / 256.0
    mean = lax.optimization_barrier(jnp.mean(score, axis=1, keepdims=True))
    spread = jnp.sqrt(lax.optimization_barrier(jnp.mean((score - mean) ** 2, axis=1, keepdims=True)))
    weight = task_weights[task_ids][:, None]
    coefs = (score - mean) / jnp.maximum(spread, 1.0) * weight / resp_lengths.astype(jnp.float32)

    def one_prompt(items):
        q_p, rk_p, rv_p, pk_p, pv_p, out_p, go_p, lse_p, live_p, len_p, coef_p = items

        def one_group(carry, inner):
            q_g, rk_g, rv_g, out_g, go_g, lse_g, len_g, coef_g = inner
            grad_q, dpk, dpv, drk, drv = response_grads(q_g, rk_g, rv_g, pk_p, pv_p, out_g, go_g, lse_g, live_p, len_g, coef_g)
            return ((carry[0] + dpk, carry[1] + dpv), (grad_q, drk.astype(jnp.bfloat16), drv.astype(jnp.bfloat16)))
        zeros = jnp.zeros(pk_p.shape, jnp.float32)
        sums, outs = lax.scan(one_group, (zeros, zeros), (q_p, rk_p, rv_p, out_p, go_p, lse_p, len_p, coef_p))
        return (outs[0], outs[1], outs[2], sums[0].astype(jnp.bfloat16), sums[1].astype(jnp.bfloat16))
    result = lax.map(one_prompt, (queries, resp_keys, resp_values, prompt_keys, prompt_values, attn_out, grad_out, log_sums, prompt_lengths, resp_lengths, coefs))
    return (result[0], result[1], result[2], result[3], result[4])
```

```python
import functools
import math

import jax
import jax.numpy as jnp
from jax import lax
from jax.experimental import pallas as pl
from jax.experimental.pallas import tpu as pltpu
from jax.sharding import PartitionSpec as P

HEADS = 4
QPK = 8
HD = 128
SHARD = 48
ROWS = HEADS * SHARD
KV = 2 * ROWS
PAY = KV + 16
RING = 8
PAIR = 2
SCALE = HD ** (-0.5)
LOG2E = math.log2(math.e)
DEAD = 1e30
NT = (((1,), (1,)), ((), ()))
NN = (((1,), (0,)), ((), ()))
TN = (((0,), (0,)), ((), ()))
F32, BF16 = jnp.float32, jnp.bfloat16


def dot(a, b, dims):
    return lax.dot_general(a, b, dims, preferred_element_type=F32)


def params(mib):
    return pltpu.CompilerParams(vmem_limit_bytes=mib << 20, dimension_semantics=("arbitrary",))


def cost(flops, traffic):
    return pl.CostEstimate(flops=flops, bytes_accessed=traffic, transcendentals=0)


def resp_body(step, q_ref, go_ref, ao_ref, lse_ref, rk_ref, rv_ref, del_ref, ds_ref, dk_ref, dv_ref):
    rows = q_ref.shape[0] * QPK
    tb = step // QPK
    ones = jnp.ones((8, HD), BF16)
    for i in reversed(range(rows // step)):
        tok = pl.ds(i * tb, tb)
        cols = pl.ds(i * step, step)
        seen = (i + 1) * tb
        q = q_ref[tok].reshape(step, HD)
        go = go_ref[tok].reshape(step, HD)
        prod = go.astype(F32) * ao_ref[tok].reshape(step, HD).astype(F32)
        high = prod.astype(BF16)
        low = (prod - high.astype(F32)).astype(BF16)
        delta = (dot(ones, high, NT) + dot(ones, low, NT))[0:1]
        del_ref[0, :, cols] = delta
        k, v = rk_ref[0, :seen], rv_ref[0, :seen]
        s = dot(k, q, NT) * (SCALE * LOG2E) - lse_ref[0, :, cols]
        key = lax.broadcasted_iota(jnp.int32, (seen, step), 0)
        query = i * tb + lax.broadcasted_iota(jnp.int32, (seen, step), 1) // QPK
        p = jnp.where(key <= query, jnp.exp2(s), 0.0)
        ds = p * (dot(v, go, NT) - delta)
        pb, dsb = p.astype(BF16), ds.astype(BF16)
        ds_ref[0, :seen, cols] = dsb
        if seen < ds_ref.shape[1]:
            ds_ref[0, seen:, cols] = jnp.zeros((ds_ref.shape[1] - seen, step), BF16)
            dk_ref[0, :seen] += dot(dsb, q, NN)
            dv_ref[0, :seen] += dot(pb, go, NN)
        else:
            dk_ref[0] = dot(dsb, q, NN)
            dv_ref[0] = dot(pb, go, NN)


def resp_grads(q, go, ao, lse, rk, rv):
    toks = q.shape[0]
    rows = toks * QPK
    per_head = pl.BlockSpec((toks, QPK, HD), lambda h: (0, h, 0))
    row = pl.BlockSpec((1, 1, rows), lambda h: (h, 0, 0))
    keys = pl.BlockSpec((1, toks, HD), lambda h: (h, 0, 0))
    return pl.pallas_call(
        functools.partial(resp_body, 512),
        grid=(HEADS,),
        in_specs=[per_head, per_head, per_head, row, keys, keys],
        out_specs=[row, pl.BlockSpec((1, toks, rows), lambda h: (h, 0, 0)), keys, keys],
        out_shape=[
            jax.ShapeDtypeStruct((HEADS, 1, rows), F32),
            jax.ShapeDtypeStruct((HEADS, toks, rows), BF16),
            jax.ShapeDtypeStruct((HEADS, toks, HD), F32),
            jax.ShapeDtypeStruct((HEADS, toks, HD), F32),
        ],
        compiler_params=params(40),
        cost_estimate=cost(6 * 10**9, 12 * 10**6),
        name="resp",
    )(q, go, ao, lse, rk, rv)


def shard_keys(refs, h):
    k, v = [], []
    for r in refs:
        for at in range(0, r.shape[0], PAY):
            k.append(r[pl.ds(pl.multiple_of(at + h * SHARD, 16), SHARD)])
            v.append(r[pl.ds(pl.multiple_of(at + ROWS + h * SHARD, 16), SHARD)])
    return jnp.concatenate(k, 0), jnp.concatenate(v, 0)


def shard_rewards(refs):
    got = []
    for r in refs:
        for at in range(0, r.shape[0], PAY):
            tail = r[pl.ds(at + KV, 16)].astype(F32)
            got.append((tail[0:1] * 32.0 + tail[1:2], tail[2:3]))
    return got


def prompt_body(step, n, own, notes, last, q_ref, go_ref, lse_ref, del_ref, *refs):
    stat_in = refs[0]
    aux = refs[1] if last else None
    refs = refs[2:] if last else refs[1:]
    kv, (ds_ref, own_ref, oth_ref, stat_ref) = refs[:n], refs[n:]
    h = pl.program_id(0)
    rows = q_ref.shape[0] * QPK
    tb = step // QPK
    got = shard_rewards(kv)
    total, square = stat_in[0:1], stat_in[1:2]
    for r, _ in got:
        total, square = total + r, square + r * r
    stat_ref[...] = stat_in[...]
    stat_ref[0:1], stat_ref[1:2] = total, square
    for at, which in notes:
        stat_ref[at : at + 1], stat_ref[at + 1 : at + 2] = got[which]
    factor = None
    if last:
        members = float(RING * PAIR)
        whole, pairs = total.astype(jnp.int32), square.astype(jnp.int32)
        spare = (RING * PAIR * pairs - whole * whole).astype(F32)
        spread = jnp.sqrt(jnp.maximum(spare, 0.0)) * (1.0 / (members * 256.0))
        weight = aux[2:3] / jnp.maximum(spread, 1.0)
        coefs = []
        for r, length in [(aux[0:1], aux[1:2])] + [
            (stat_in[at : at + 1], stat_in[at + 1 : at + 2]) for at in (2, 4, 6)
        ]:
            coefs.append((r * members - total) * (1.0 / (members * 256.0)) * weight / length)
        for at, c in enumerate(coefs):
            stat_ref[at : at + 1] = c
        factor = coefs[0]
    k, v = shard_keys(kv, h)
    dk = dv = None
    for i in range(rows // step):
        tok = pl.ds(i * tb, tb)
        cols = pl.ds(i * step, step)
        q = q_ref[tok].reshape(step, HD)
        go = go_ref[tok].reshape(step, HD)
        p = jnp.exp2(dot(k, q, NT) * (SCALE * LOG2E) - lse_ref[0, :, cols])
        ds = p * (dot(v, go, NT) - del_ref[0, :, cols])
        pb, dsb = p.astype(BF16), ds.astype(BF16)
        ds_ref[0, :, cols] = dsb
        a, b = dot(dsb, q, NN), dot(pb, go, NN)
        dk, dv = (a, b) if dk is None else (dk + a, dv + b)
    dk = dk * SCALE
    if last:
        dk, dv = dk * factor, dv * factor
    slots = [0, 0]
    for at, mine in enumerate(own):
        out = own_ref if mine else oth_ref
        to = slots[0 if mine else 1]
        slots[0 if mine else 1] += 1
        out[to, 0, 0] = dk[at * SHARD : (at + 1) * SHARD].astype(BF16)
        out[to, 1, 0] = dv[at * SHARD : (at + 1) * SHARD].astype(BF16)


def prompt_grads(name, q, go, lse, delta, stat, aux, shards, own, notes, last):
    toks = q.shape[0]
    rows = toks * QPK
    keys = len(own) * SHARD
    half = len(own) // 2
    per_head = pl.BlockSpec((toks, QPK, HD), lambda h: (0, h, 0))
    row = pl.BlockSpec((1, 1, rows), lambda h: (h, 0, 0))
    small = pl.BlockSpec((8, HD), lambda h: (0, 0))
    grad = pl.BlockSpec((half, 2, 1, SHARD, HD), lambda h: (0, 0, h, 0, 0))
    extra = [aux] if last else []
    return pl.pallas_call(
        functools.partial(prompt_body, 1024, len(shards), own, notes, last),
        grid=(HEADS,),
        in_specs=[per_head, per_head, row, row, small]
        + [small] * len(extra)
        + [pl.BlockSpec(s.shape, lambda h: (0, 0)) for s in shards],
        out_specs=[pl.BlockSpec((1, keys, rows), lambda h: (h, 0, 0)), grad, grad, small],
        out_shape=[
            jax.ShapeDtypeStruct((HEADS, keys, rows), BF16),
            jax.ShapeDtypeStruct((half, 2, HEADS, SHARD, HD), BF16),
            jax.ShapeDtypeStruct((half, 2, HEADS, SHARD, HD), BF16),
            jax.ShapeDtypeStruct((8, HD), F32),
        ],
        compiler_params=params(40),
        cost_estimate=cost(keys * 25 * 10**6, 8 * 10**6),
        name=name,
    )(q, go, lse, delta, stat, *extra, *shards)


def query_body(step, head, n_ds, counts, coef_ref, *refs):
    ds, refs = refs[:n_ds], refs[n_ds:]
    shards, rk_ref, out = refs[: sum(counts)], refs[sum(counts)], refs[-1]
    rows = out.shape[0] * QPK
    keys, at = [], 0
    for c in counts:
        keys.append(shard_keys(shards[at : at + c], head)[0])
        at += c
    keys.append(rk_ref[0])
    factor = coef_ref[0:1] * SCALE
    for i in range(rows // step):
        cols = pl.ds(i * step, step)
        acc = None
        for d, k in zip(ds, keys):
            a = dot(k, d[0, :, cols], TN)
            acc = a if acc is None else acc + a
        out[pl.ds(i * step // QPK, step // QPK)] = (
            (acc.T * factor).astype(BF16).reshape(step // QPK, QPK, HD)
        )


def query_grads(head, coef, ds, groups, rk, so_far, toks):
    rows = toks * QPK
    counts = [len(g) for g in groups]
    shards = [s for g in groups for s in g]
    small = pl.BlockSpec((8, HD), lambda i: (0, 0))
    body = functools.partial(query_body, 512, head, len(ds), counts)
    ins = [coef, *ds, *shards, rk]
    specs = (
        [small]
        + [pl.BlockSpec((1, d.shape[1], rows), lambda i: (head, 0, 0)) for d in ds]
        + [pl.BlockSpec(s.shape, lambda i: (0, 0)) for s in shards]
        + [pl.BlockSpec((1, toks, HD), lambda i: (head, 0, 0))]
    )
    alias = {}
    if so_far is not None:
        alias = {len(ins): 0}
        ins.append(so_far)
        specs.append(pl.BlockSpec(memory_space=pl.ANY))
        inner = body
        body = lambda *refs: inner(*refs[:-2], refs[-1])
    return pl.pallas_call(
        body,
        grid=(1,),
        in_specs=specs,
        out_specs=pl.BlockSpec((toks, QPK, HD), lambda i: (0, head, 0)),
        out_shape=jax.ShapeDtypeStruct((toks, HEADS * QPK, HD), BF16),
        input_output_aliases=alias,
        compiler_params=params(40),
        cost_estimate=cost(25 * 10**8, 5 * 10**6),
        name="dq",
    )(*ins)


def hop(x, dz, dy=0):
    pairs = [
        (z * PAIR + y, ((z + dz) % RING) * PAIR + (y + dy) % PAIR)
        for z in range(RING)
        for y in range(PAIR)
    ]
    return lax.ppermute(x, "group", pairs)


def swap_core(x):
    return lax.ppermute(x, "tensor", [(0, 1), (1, 0)])


def in_order(core, mine, other, axis):
    return jnp.where(
        core == 0,
        jnp.concatenate([mine, other], axis),
        jnp.concatenate([other, mine], axis),
    )


def on_device(
    queries,
    resp_keys,
    resp_values,
    prompt_keys,
    prompt_values,
    attn_out,
    grad_out,
    log_sums,
    prompt_lengths,
    resp_lengths,
    rewards,
    task_ids,
    task_weights,
):
    core = lax.axis_index("tensor")
    member = lax.axis_index("group")
    toks = queries.shape[2]
    rows = toks * QPK
    part = prompt_keys.shape[1]
    live = prompt_lengths[0]
    length = resp_lengths[0, 0]
    reward = rewards[0, 0]

    slot = (member * 2 + core) * part + jnp.arange(part)
    alive = (slot < live)[:, None, None]
    both = jnp.stack([jnp.where(alive, prompt_keys[0], 0), prompt_values[0]])
    both = both.reshape(2, part, 2, HEADS, HD).transpose(2, 0, 3, 1, 4)
    mine = lax.dynamic_index_in_dim(both, core, 0, keepdims=False)
    theirs = lax.dynamic_index_in_dim(both, 1 - core, 0, keepdims=False)
    got = swap_core(theirs)
    shard = in_order(core, mine, got, 2).reshape(KV, HD)
    line = jnp.arange(16)[:, None]
    note = jnp.where(line == 0, reward // 32, jnp.where(line == 1, reward % 32, length))
    own = jnp.concatenate([shard, jnp.broadcast_to(note, (16, HD)).astype(BF16)], 0)

    east, west = hop(own, 1), hop(own, -1)
    beside = hop(own, 0, 1)
    east_x, west_x = hop(own, 1, 1), hop(own, -1, 1)
    far = hop(own, 4)
    back1, fore1 = jnp.concatenate([east, east_x], 0), jnp.concatenate([west, west_x], 0)
    back2, fore2 = hop(back1, 1), hop(fore1, -1)
    far_x = hop(far, 0, 1)
    back3, fore3 = hop(back2, 1), hop(fore2, -1)

    q = queries[0, 0].reshape(toks, HEADS * QPK, HD)
    go = grad_out[0, 0].reshape(toks, HEADS * QPK, HD)
    ao = attn_out[0, 0].reshape(toks, HEADS * QPK, HD)
    rk = resp_keys[0, 0].transpose(1, 0, 2)
    rv = resp_values[0, 0].transpose(1, 0, 2)
    lse = log_sums[0, 0].transpose(0, 2, 1) * LOG2E
    lse = jnp.where((jnp.arange(toks) < length)[None, :, None], lse, DEAD).reshape(HEADS, 1, rows)
    weight = jnp.sum(jnp.where(jnp.arange(task_weights.shape[0]) == task_ids[0], task_weights, 0.0))
    line = jnp.arange(8)[:, None]
    aux = jnp.where(line == 0, reward.astype(F32), jnp.where(line == 1, length.astype(F32), weight))
    aux = jnp.broadcast_to(aux, (8, HD))
    stat = jnp.zeros((8, HD), F32)

    delta, ds_r, dk_r, dv_r = resp_grads(q, go, ao, lse, rk, rv)
    near = [own, beside, back1, fore1]
    mix = (True, False)
    ds_1, own_1, oth_1, stat = prompt_grads(
        "near", q, go, lse, delta, stat, None, near, mix * 3, ((2, 1),), False
    )
    ds_2, own_2, oth_2, stat = prompt_grads(
        "second", q, go, lse, delta, stat, None, [back2, fore2], mix * 2, (), False
    )
    ds_4, own_4, oth_4, stat = prompt_grads(
        "far", q, go, lse, delta, stat, None, [far, far_x], mix, ((4, 0), (6, 1)), False
    )
    ds_3, own_3, oth_3, coef = prompt_grads(
        "third", q, go, lse, delta, stat, aux, [back3, fore3], mix * 2, (), True
    )

    def flat(x):
        return x.reshape(x.shape[0], KV, HD)

    own_1, oth_1, own_2, oth_2 = flat(own_1), flat(oth_1), flat(own_2), flat(oth_2)
    own_3, oth_3, own_4, oth_4 = flat(own_3), flat(oth_3), flat(own_4), flat(oth_4)
    side_1, side_2 = hop(oth_1, 0, 1), hop(oth_2, 0, 1)
    far_own, far_oth = hop(own_4[0], 4), hop(oth_4[0], 4, 1)
    mine_c, side_c, far_c, farx_c = coef[0:1], coef[1:2], coef[2:3], coef[3:4]

    def term(own_n, side_n, at):
        return mine_c * own_n[at].astype(F32) + side_c * side_n[at].astype(F32)

    down = hop(own_3[0], -1).astype(F32) + hop(oth_3[0], -1, 1).astype(F32)
    up = hop(own_3[1], 1).astype(F32) + hop(oth_3[1], 1, 1).astype(F32)
    down = hop((down + term(own_2, side_2, 0)).astype(BF16), -1).astype(F32)
    up = hop((up + term(own_2, side_2, 1)).astype(BF16), 1).astype(F32)
    down = hop((down + term(own_1, side_1, 1)).astype(BF16), -1).astype(F32)
    up = hop((up + term(own_1, side_1, 2)).astype(BF16), 1).astype(F32)
    home = term(own_1, side_1, 0) + far_c * far_own.astype(F32) + farx_c * far_oth.astype(F32)
    home = (home + down + up).astype(BF16).reshape(2, HEADS, 2, part, HD)
    keep = lax.dynamic_index_in_dim(home, core, 2, keepdims=False)
    give = lax.dynamic_index_in_dim(home, 1 - core, 2, keepdims=False)
    take = swap_core(give)
    done = in_order(core, keep, take, 1).transpose(0, 2, 1, 3)
    done = jnp.where(alive[None], done, 0)

    groups = [near, [back2, fore2], [far, far_x], [back3, fore3]]
    grad_q = None
    for head in range(HEADS):
        grad_q = query_grads(
            head, coef, [ds_1, ds_2, ds_4, ds_3, ds_r], groups, rk, grad_q, toks
        )
    own_scale = coef[0, 0]
    drk = (dk_r * (own_scale * SCALE)).astype(BF16).transpose(1, 0, 2)
    drv = (dv_r * own_scale).astype(BF16).transpose(1, 0, 2)
    return (
        grad_q.reshape(1, 1, toks, HEADS, QPK, HD),
        drk[None, None],
        drv[None, None],
        done[0][None],
        done[1][None],
    )


def solution(mesh):
    wide = P("prompt", "group", None, "tensor", None, None)
    resp = P("prompt", "group", None, "tensor", None)
    prompt = P("prompt", ("group", "tensor"), None, None)
    return jax.shard_map(
        on_device,
        mesh=mesh,
        in_specs=(
            wide,
            resp,
            resp,
            prompt,
            prompt,
            wide,
            wide,
            P("prompt", "group", "tensor", None, None),
            P("prompt"),
            P("prompt", "group"),
            P("prompt", "group"),
            P("prompt"),
            P(),
        ),
        out_specs=(wide, resp, resp, prompt, prompt),
        check_vma=False,
    )
```

```python
import functools
import math

import jax
import jax.numpy as jnp
from jax import lax
from jax.experimental import pallas as pl
from jax.experimental.pallas import tpu as pltpu
from jax.sharding import PartitionSpec as P

HEADS = 4
QPK = 8
HD = 128
SHARD = 48
ROWS = HEADS * SHARD
KV = 2 * ROWS
PAY = KV + 16
RING = 8
PAIR = 2
SCALE = HD ** (-0.5)
LOG2E = math.log2(math.e)
DEAD = 1e30
WHOLE = pl.BlockSpec(memory_space=pltpu.VMEM)
GRANT = 20
SMALL = 4
NT = (((1,), (1,)), ((), ()))
NN = (((1,), (0,)), ((), ()))
TN = (((0,), (0,)), ((), ()))
F32, BF16 = jnp.float32, jnp.bfloat16


def dot(a, b, dims):
    return lax.dot_general(a, b, dims, preferred_element_type=F32)


def cost(flops, traffic):
    return pl.CostEstimate(flops=flops, bytes_accessed=traffic, transcendentals=0)


def split_body(live_ref, pk_ref, pv_ref, mine_ref, theirs_ref):
    core, member = lax.axis_index("tensor"), lax.axis_index("group")
    part = pk_ref.shape[1]
    slot = (member * 2 + core) * part + lax.broadcasted_iota(jnp.int32, pk_ref.shape[1:], 0)
    keys = jnp.where(slot < live_ref[0], pk_ref[0].astype(F32), 0.0)
    for at, x in enumerate((keys, pv_ref[0].astype(F32))):
        x = jnp.transpose(x, (1, 0, 2))
        low, high = x[:HEADS], x[HEADS:]
        mine_ref[at] = jnp.where(core == 0, low, high)
        theirs_ref[at] = jnp.where(core == 0, high, low)


def split_heads(live, pk, pv):
    part = pk.shape[1]
    whole = pl.BlockSpec(memory_space=pltpu.VMEM)
    half = jax.ShapeDtypeStruct((2, HEADS, part, HD), F32)
    return pl.pallas_call(
        split_body,
        in_specs=[pl.BlockSpec(memory_space=pltpu.SMEM), whole, whole],
        out_specs=[whole, whole],
        out_shape=[half, half],
        compiler_params=pltpu.CompilerParams(vmem_limit_bytes=SMALL << 20),
        name="split",
    )(live, pk, pv)


def join_body(reward_ref, length_ref, mine_ref, got_ref, out_ref):
    core = lax.axis_index("tensor")
    for at in range(2):
        for h in range(HEADS):
            a, b = mine_ref[at, h], got_ref[at, h]
            pair = [jnp.where(core == 0, a, b), jnp.where(core == 0, b, a)]
            first = (at * HEADS + h) * SHARD
            out_ref[first : first + SHARD] = jnp.concatenate(pair, 0).astype(BF16)
    reward, length = reward_ref[0, 0], length_ref[0, 0]
    line = lax.broadcasted_iota(jnp.int32, (16, HD), 0)
    note = jnp.where(line == 0, reward >> 5, jnp.where(line == 1, reward & 31, length))
    out_ref[KV:] = note.astype(F32).astype(BF16)


def join_tokens(reward, length, mine, got):
    whole = pl.BlockSpec(memory_space=pltpu.VMEM)
    number = pl.BlockSpec(memory_space=pltpu.SMEM)
    return pl.pallas_call(
        join_body,
        in_specs=[number, number, whole, whole],
        out_specs=whole,
        out_shape=jax.ShapeDtypeStruct((PAY, HD), BF16),
        compiler_params=pltpu.CompilerParams(vmem_limit_bytes=SMALL << 20),
        name="join",
    )(reward, length, mine, got)


def pair_body(wait_ref, own_ref, beside_ref, out_ref):
    out_ref[:PAY] = own_ref[...]
    out_ref[PAY:] = beside_ref[...]


def join_pair(wait, own, beside):
    return pl.pallas_call(
        pair_body,
        in_specs=[pl.BlockSpec(memory_space=pl.ANY), WHOLE, WHOLE],
        out_specs=WHOLE,
        out_shape=jax.ShapeDtypeStruct((PAIR * PAY, HD), BF16),
        compiler_params=pltpu.CompilerParams(vmem_limit_bytes=SMALL << 20),
        name="pair",
    )(wait, own, beside)


def rows_body(length_ref, wait_ref, rk_ref, rv_ref, lse_ref, rkt_ref, rvt_ref, row_ref):
    toks = rk_ref.shape[0]
    rows = toks * QPK
    for src, dst in ((rk_ref, rkt_ref), (rv_ref, rvt_ref)):
        dst[...] = jnp.transpose(src[...].astype(F32), (1, 0, 2)).astype(BF16)
    spread = lax.broadcasted_iota(jnp.int32, (toks, rows), 1) // QPK
    spread = (spread == lax.broadcasted_iota(jnp.int32, (toks, rows), 0)).astype(BF16)
    parts = []
    for h in range(HEADS):
        x = lse_ref[h] * LOG2E
        for _ in range(3):
            parts.append(x.astype(BF16))
            x = x - parts[-1].astype(F32)
    wide = dot(jnp.concatenate(parts, 0), spread, NN)
    line = lax.broadcasted_iota(jnp.int32, (QPK, rows), 0)
    lane = lax.broadcasted_iota(jnp.int32, (QPK, rows), 1)
    for h in range(HEADS):
        at = h * 3 * QPK
        x = wide[at : at + QPK] + (wide[at + QPK : at + 2 * QPK] + wide[at + 2 * QPK : at + 3 * QPK])
        x = jnp.sum(jnp.where(lane % QPK == line, x, 0.0), axis=0, keepdims=True)
        row_ref[h] = jnp.where(lane[0:1] // QPK < length_ref[0, 0], x, DEAD)


def resp_rows(length, wait, rk, rv, lse):
    toks = rk.shape[0]
    by_head = jax.ShapeDtypeStruct((HEADS, toks, HD), BF16)
    return pl.pallas_call(
        rows_body,
        in_specs=[pl.BlockSpec(memory_space=pltpu.SMEM), pl.BlockSpec(memory_space=pl.ANY)]
        + [WHOLE] * 3,
        out_specs=[WHOLE] * 3,
        out_shape=[by_head, by_head, jax.ShapeDtypeStruct((HEADS, 1, toks * QPK), F32)],
        compiler_params=pltpu.CompilerParams(vmem_limit_bytes=GRANT << 20),
        cost_estimate=cost(5 * 10**9, 1 << 20),
        name="rows",
    )(length, wait, rk, rv, lse)


def loop(body):
    lax.fori_loop(0, HEADS, lambda h, c: (body(h), c)[1], 0)


def resp_body(step, q_ref, go_ref, ao_ref, lse_ref, rk_ref, rv_ref, del_ref, ds_ref, dk_ref, dv_ref):
    toks = q_ref.shape[0]
    tb = step // QPK
    ones = jnp.ones((8, HD), BF16)

    def head(h):
        for i in reversed(range(toks // tb)):
            tok = pl.ds(i * tb, tb)
            cols = pl.ds(i * step, step)
            seen = (i + 1) * tb
            q = q_ref[tok, h].reshape(step, HD)
            go = go_ref[tok, h].reshape(step, HD)
            prod = go.astype(F32) * ao_ref[tok, h].reshape(step, HD).astype(F32)
            high = prod.astype(BF16)
            low = (prod - high.astype(F32)).astype(BF16)
            delta = (dot(ones, high, NT) + dot(ones, low, NT))[0:1]
            del_ref[h, :, cols] = delta
            k, v = rk_ref[h, :seen], rv_ref[h, :seen]
            s = dot(k, q, NT) * (SCALE * LOG2E) - lse_ref[h, :, cols]
            key = lax.broadcasted_iota(jnp.int32, (seen, step), 0)
            query = i * tb + lax.broadcasted_iota(jnp.int32, (seen, step), 1) // QPK
            p = jnp.where(key <= query, jnp.exp2(s), 0.0)
            ds = p * (dot(v, go, NT) - delta)
            pb, dsb = p.astype(BF16), ds.astype(BF16)
            ds_ref[h, :seen, cols] = dsb
            if seen < toks:
                ds_ref[h, seen:, cols] = jnp.zeros((toks - seen, step), BF16)
                dk_ref[h, :seen] += dot(dsb, q, NN)
                dv_ref[h, :seen] += dot(pb, go, NN)
            else:
                dk_ref[h] = dot(dsb, q, NN)
                dv_ref[h] = dot(pb, go, NN)

    loop(head)


def resp_grads(q, go, ao, lse, rk, rv):
    toks = q.shape[0]
    rows = toks * QPK
    return pl.pallas_call(
        functools.partial(resp_body, 512),
        in_specs=[WHOLE] * 6,
        out_specs=[WHOLE] * 4,
        out_shape=[
            jax.ShapeDtypeStruct((HEADS, 1, rows), F32),
            jax.ShapeDtypeStruct((HEADS, toks, rows), BF16),
            jax.ShapeDtypeStruct((HEADS, toks, HD), F32),
            jax.ShapeDtypeStruct((HEADS, toks, HD), F32),
        ],
        compiler_params=pltpu.CompilerParams(vmem_limit_bytes=GRANT << 20),
        cost_estimate=cost(5 * 10**9, 1 << 20),
        name="resp",
    )(q, go, ao, lse, rk, rv)


def shard_keys(refs, h):
    k, v = [], []
    for r in refs:
        for at in range(0, r.shape[0], PAY):
            k.append(r[pl.ds(pl.multiple_of(at + h * SHARD, 16), SHARD)])
            v.append(r[pl.ds(pl.multiple_of(at + ROWS + h * SHARD, 16), SHARD)])
    return jnp.concatenate(k, 0), jnp.concatenate(v, 0)


def shard_rewards(refs):
    got = []
    for r in refs:
        for at in range(0, r.shape[0], PAY):
            tail = r[pl.ds(at + KV, 16)].astype(F32)
            got.append((tail[0:1] * 32.0 + tail[1:2], tail[2:3]))
    return got


def prompt_body(step, n, note, last, q_ref, go_ref, lse_ref, del_ref, stat_in, *refs):
    aux = refs[0] if last else None
    refs = refs[1:] if last else refs
    kv, ds_ref, outs, stat_ref = refs[:n], refs[n], refs[n + 1 : 2 * n + 1], refs[2 * n + 1]
    toks = q_ref.shape[0]
    tb = step // QPK
    got = shard_rewards(kv)
    total, square = stat_in[0:1], stat_in[1:2]
    for r, _ in got:
        total, square = total + r, square + r * r
    stat_ref[...] = stat_in[...]
    stat_ref[0:1], stat_ref[1:2] = total, square
    if note:
        stat_ref[2:3], stat_ref[3:4] = got[0]
    factor = None
    if last:
        members = float(RING * PAIR)
        whole, pairs = total.astype(jnp.int32), square.astype(jnp.int32)
        spare = (RING * PAIR * pairs - whole * whole).astype(F32)
        spread = jnp.sqrt(jnp.maximum(spare, 0.0)) * (1.0 / (members * 256.0))
        weight = aux[2:3] / jnp.maximum(spread, 1.0)
        coefs = []
        for r, length in ((aux[0:1], aux[1:2]), (stat_in[2:3], stat_in[3:4])):
            coefs.append((r * members - total) * (1.0 / (members * 256.0)) * weight / length)
        stat_ref[0:1], stat_ref[1:2] = coefs
        factor = coefs[0]

    def head(h):
        k, v = shard_keys(kv, h)
        dk = dv = None
        for i in range(toks // tb):
            tok = pl.ds(i * tb, tb)
            cols = pl.ds(i * step, step)
            q = q_ref[tok, h].reshape(step, HD)
            go = go_ref[tok, h].reshape(step, HD)
            p = jnp.exp2(dot(k, q, NT) * (SCALE * LOG2E) - lse_ref[h, :, cols])
            ds = p * (dot(v, go, NT) - del_ref[h, :, cols])
            pb, dsb = p.astype(BF16), ds.astype(BF16)
            ds_ref[h, :, cols] = dsb
            a, b = dot(dsb, q, NN), dot(pb, go, NN)
            dk, dv = (a, b) if dk is None else (dk + a, dv + b)
        dk = dk * SCALE
        if last:
            dk, dv = dk * factor, dv * factor
        at = 0
        for out in outs:
            for y in range(PAIR):
                out[y, 0, h] = dk[at : at + SHARD].astype(BF16)
                out[y, 1, h] = dv[at : at + SHARD].astype(BF16)
                at += SHARD

    loop(head)


def prompt_grads(name, q, go, lse, delta, stat, aux, shards, note, last):
    rows = q.shape[0] * QPK
    keys = len(shards) * PAIR * SHARD
    extra = [aux] if last else []
    ins = [q, go, lse, delta, stat, *extra, *shards]
    pair = jax.ShapeDtypeStruct((PAIR, 2, HEADS, SHARD, HD), BF16)
    got = pl.pallas_call(
        functools.partial(prompt_body, 1024, len(shards), note, last),
        in_specs=[WHOLE] * len(ins),
        out_specs=[WHOLE] * (len(shards) + 2),
        out_shape=[
            jax.ShapeDtypeStruct((HEADS, keys, rows), BF16),
            *[pair] * len(shards),
            jax.ShapeDtypeStruct((8, HD), F32),
        ],
        compiler_params=pltpu.CompilerParams(vmem_limit_bytes=GRANT << 20),
        cost_estimate=cost((keys // 192) * 5 * 10**9 + 10**8, 1 << 20),
        name=name,
    )(*ins)
    return got[0], [x.reshape(PAIR * KV, HD) for x in got[1:-1]], got[-1]


def query_body(head, n_ds, counts, ins, coef_ref, *refs):
    ds, shards, rk_ref = refs[:n_ds], refs[n_ds : n_ds + sum(counts)], refs[n_ds + sum(counts)]
    out, coef_out, rows_ref, sems = refs[ins - 1 :]
    step = 512
    tb = step // QPK
    keys, at = [], 0
    for c in counts:
        keys.append(shard_keys(shards[at : at + c], head)[0])
        at += c
    keys.append(rk_ref[head])
    coef_out[...] = coef_ref[...]
    factor = coef_ref[0:1] * SCALE
    sends = []
    for i in range(ds[0].shape[2] // step):
        acc = None
        for d, k in zip(ds, keys):
            a = dot(k, d[head, :, pl.ds(i * step, step)], TN)
            acc = a if acc is None else acc + a
        rows_ref[i * tb : (i + 1) * tb] = (acc.T * factor).astype(BF16).reshape(tb, QPK, HD)
        tok = pl.ds(i * tb, tb)
        sends.append(pltpu.make_async_copy(rows_ref.at[tok], out.at[tok, head], sems.at[i]))
        sends[-1].start()
    for send in sends:
        send.wait()


def query_grads(head, coef, ds, groups, rk, so_far, *waits):
    toks = ds[0].shape[2] // QPK
    counts = [len(g) for g in groups]
    shards = [s for g in groups for s in g]
    there = pl.BlockSpec(memory_space=pl.ANY)
    ins = [coef, *ds, *shards, rk]
    specs = [WHOLE] * len(ins) + [there] * len(waits)
    ins += waits
    alias = {}
    if so_far is not None:
        alias = {len(ins): 0}
        ins.append(so_far)
        specs.append(there)
    return pl.pallas_call(
        functools.partial(query_body, head, len(ds), counts, len(ins)),
        in_specs=specs,
        out_specs=[there, WHOLE],
        out_shape=[
            jax.ShapeDtypeStruct((toks, HEADS, QPK, HD), BF16),
            jax.ShapeDtypeStruct((8, HD), F32),
        ],
        input_output_aliases=alias,
        scratch_shapes=[pltpu.VMEM((toks, QPK, HD), BF16), pltpu.SemaphoreType.DMA((4,))],
        compiler_params=pltpu.CompilerParams(vmem_limit_bytes=GRANT << 20),
        cost_estimate=cost(4 * 10**9, 1 << 20),
        name="dq",
    )(*ins)


def hop(x, dz, dy=0):
    pairs = [
        (z * PAIR + y, ((z + dz) % RING) * PAIR + (y + dy) % PAIR)
        for z in range(RING)
        for y in range(PAIR)
    ]
    return lax.ppermute(x, "group", pairs)


def swap_core(x):
    return lax.ppermute(x, "tensor", [(0, 1), (1, 0)])


def in_order(core, mine, other, axis):
    return jnp.where(
        core == 0,
        jnp.concatenate([mine, other], axis),
        jnp.concatenate([other, mine], axis),
    )


def on_device(
    queries,
    resp_keys,
    resp_values,
    prompt_keys,
    prompt_values,
    attn_out,
    grad_out,
    log_sums,
    prompt_lengths,
    resp_lengths,
    rewards,
    task_ids,
    task_weights,
):
    core = lax.axis_index("tensor")
    member = lax.axis_index("group")
    toks = queries.shape[2]
    part = prompt_keys.shape[1]
    length = resp_lengths[0, 0]
    reward = rewards[0, 0]

    mine, theirs = split_heads(prompt_lengths, prompt_keys, prompt_values)
    own = join_tokens(rewards, resp_lengths, mine, swap_core(theirs))

    q, go, ao = queries[0, 0], grad_out[0, 0], attn_out[0, 0]
    rk, rv, lse = resp_rows(
        resp_lengths, own, resp_keys[0, 0], resp_values[0, 0], log_sums[0, 0]
    )
    length = resp_lengths[0, 0]
    weight = jnp.sum(jnp.where(jnp.arange(task_weights.shape[0]) == task_ids[0], task_weights, 0.0))
    line = jnp.arange(8)[:, None]
    reward = rewards[0, 0].astype(F32)
    aux = jnp.where(line == 0, reward, jnp.where(line == 1, length.astype(F32), weight))
    aux = jnp.broadcast_to(aux, (8, HD))
    stat = jnp.zeros((8, HD), F32)

    delta, ds_r, dk_r, dv_r = resp_grads(q, go, ao, lse, rk, rv)
    pair = join_pair(lse, own, hop(own, 0, 1))
    back1, fore1 = hop(pair, 1), hop(pair, -1)
    far = hop(pair, 4)
    back2, fore2 = hop(back1, 1), hop(fore1, -1)
    back3, fore3 = hop(back2, 1), hop(fore2, -1)

    common = (q, go, lse, delta)
    ds_1, (here, down_1, up_1), stat = prompt_grads(
        "near", *common, stat, None, [pair, back1, fore1], False, False
    )
    ds_2, (down_2, up_2), stat = prompt_grads(
        "second", *common, stat, None, [back2, fore2], False, False
    )
    ds_4, (across,), stat = prompt_grads("far", *common, stat, None, [far], True, False)
    ds_3, (down_3, up_3), coef = prompt_grads(
        "third", *common, stat, aux, [back3, fore3], False, True
    )

    groups = [[pair, back1, fore1], [back2, fore2], [far], [back3, fore3]]
    ds_all = [ds_1, ds_2, ds_4, ds_3, ds_r]

    def dq(head, so_far, *waits):
        return query_grads(head, coef, ds_all, groups, rk, so_far, *waits)

    def add(a, c, b):
        return (a.astype(F32) + c[0:1] * b.astype(F32)).astype(BF16)

    down, up = hop(down_3, -1), hop(up_3, 1)
    grad_q, _ = dq(0, None)
    grad_q, again = dq(1, grad_q)
    down, up = add(down, again, down_2), add(up, again, up_2)
    far_term = hop(across, 4)
    grad_q, _ = dq(2, grad_q, down, up)
    grad_q, again = dq(3, grad_q)
    down, up = hop(down, -1), hop(up, 1)
    down, up = add(down, again, down_1), add(up, again, up_1)
    down, up = hop(down, -1), hop(up, 1)
    home = coef[0:1] * here.astype(F32) + coef[1:2] * far_term.astype(F32)
    home = home + down.astype(F32) + up.astype(F32)
    beside = hop(home[KV:].astype(BF16), 0, 1)
    home = (home[:KV] + beside.astype(F32)).reshape(2, HEADS, 2, part, HD)
    keep = lax.dynamic_index_in_dim(home, core, 2, keepdims=False)
    give = lax.dynamic_index_in_dim(home, 1 - core, 2, keepdims=False)
    take = swap_core(give)
    done = in_order(core, keep, take, 1).transpose(0, 2, 1, 3).astype(BF16)
    slot = (member * 2 + core) * part + jnp.arange(part)
    done = jnp.where((slot < prompt_lengths[0])[None, :, None, None], done, 0)
    own_scale = coef[0, 0]
    drk = (dk_r * (own_scale * SCALE)).astype(BF16).transpose(1, 0, 2)
    drv = (dv_r * own_scale).astype(BF16).transpose(1, 0, 2)
    return (
        grad_q.reshape(1, 1, toks, HEADS, QPK, HD),
        drk[None, None],
        drv[None, None],
        done[0][None],
        done[1][None],
    )


def solution(mesh):
    wide = P("prompt", "group", None, "tensor", None, None)
    resp = P("prompt", "group", None, "tensor", None)
    prompt = P("prompt", ("group", "tensor"), None, None)
    return jax.shard_map(
        on_device,
        mesh=mesh,
        in_specs=(
            wide,
            resp,
            resp,
            prompt,
            prompt,
            wide,
            wide,
            P("prompt", "group", "tensor", None, None),
            P("prompt"),
            P("prompt", "group"),
            P("prompt", "group"),
            P("prompt"),
            P(),
        ),
        out_specs=(wide, resp, resp, prompt, prompt),
        check_vma=False,
    )
```

```python
import functools
import math

import jax
import jax.numpy as jnp
from jax import lax
from jax.experimental import pallas as pl
from jax.experimental.pallas import tpu as pltpu
from jax.sharding import PartitionSpec as P

HEADS = 4
QPK = 8
HD = 128
SHARD = 48
ROWS = HEADS * SHARD
KV = 2 * ROWS
PAY = KV + 16
RING = 8
PAIR = 2
SCALE = HD ** (-0.5)
LOG2E = math.log2(math.e)
DEAD = 1e30
WHOLE = pl.BlockSpec(memory_space=pltpu.VMEM)
GRANT = 20
SMALL = 4
NT = (((1,), (1,)), ((), ()))
NN = (((1,), (0,)), ((), ()))
TN = (((0,), (0,)), ((), ()))
F32, BF16 = jnp.float32, jnp.bfloat16


def dot(a, b, dims):
    return lax.dot_general(a, b, dims, preferred_element_type=F32)


def cost(flops, traffic):
    return pl.CostEstimate(flops=flops, bytes_accessed=traffic, transcendentals=0)


def split_body(live_ref, pk_ref, pv_ref, mine_ref, theirs_ref):
    core, member = lax.axis_index("tensor"), lax.axis_index("group")
    part = pk_ref.shape[1]
    slot = (member * 2 + core) * part + lax.broadcasted_iota(jnp.int32, pk_ref.shape[1:], 0)
    keys = jnp.where(slot < live_ref[0], pk_ref[0].astype(F32), 0.0)
    for at, x in enumerate((keys, pv_ref[0].astype(F32))):
        x = jnp.transpose(x, (1, 0, 2))
        low, high = x[:HEADS], x[HEADS:]
        mine_ref[at] = jnp.where(core == 0, low, high)
        theirs_ref[at] = jnp.where(core == 0, high, low)


def split_heads(live, pk, pv):
    part = pk.shape[1]
    whole = pl.BlockSpec(memory_space=pltpu.VMEM)
    half = jax.ShapeDtypeStruct((2, HEADS, part, HD), F32)
    return pl.pallas_call(
        split_body,
        in_specs=[pl.BlockSpec(memory_space=pltpu.SMEM), whole, whole],
        out_specs=[whole, whole],
        out_shape=[half, half],
        compiler_params=pltpu.CompilerParams(vmem_limit_bytes=SMALL << 20),
        name="split",
    )(live, pk, pv)


def join_body(reward_ref, length_ref, mine_ref, got_ref, out_ref):
    core = lax.axis_index("tensor")
    for at in range(2):
        for h in range(HEADS):
            a, b = mine_ref[at, h], got_ref[at, h]
            pair = [jnp.where(core == 0, a, b), jnp.where(core == 0, b, a)]
            first = (at * HEADS + h) * SHARD
            out_ref[first : first + SHARD] = jnp.concatenate(pair, 0).astype(BF16)
    reward, length = reward_ref[0, 0], length_ref[0, 0]
    line = lax.broadcasted_iota(jnp.int32, (16, HD), 0)
    note = jnp.where(line == 0, reward >> 5, jnp.where(line == 1, reward & 31, length))
    out_ref[KV:] = note.astype(F32).astype(BF16)


def join_tokens(reward, length, mine, got):
    whole = pl.BlockSpec(memory_space=pltpu.VMEM)
    number = pl.BlockSpec(memory_space=pltpu.SMEM)
    return pl.pallas_call(
        join_body,
        in_specs=[number] * 2 + [whole] * 2,
        out_specs=whole,
        out_shape=jax.ShapeDtypeStruct((PAY, HD), BF16),
        compiler_params=pltpu.CompilerParams(vmem_limit_bytes=SMALL << 20),
        name="join",
    )(reward, length, mine, got)


def pair_body(wait_ref, own_ref, beside_ref, out_ref):
    out_ref[:PAY] = own_ref[...]
    out_ref[PAY:] = beside_ref[...]


def join_pair(wait, own, beside):
    return pl.pallas_call(
        pair_body,
        in_specs=[pl.BlockSpec(memory_space=pl.ANY), WHOLE, WHOLE],
        out_specs=WHOLE,
        out_shape=jax.ShapeDtypeStruct((PAIR * PAY, HD), BF16),
        compiler_params=pltpu.CompilerParams(vmem_limit_bytes=SMALL << 20),
        name="pair",
    )(wait, own, beside)


def rows_body(reward_ref, length_ref, task_ref, weights_ref, wait_ref, rk_ref, rv_ref, lse_ref, *refs):
    rkt_ref, rvt_ref, row_ref, aux_ref = refs
    toks = rk_ref.shape[0]
    rows = toks * QPK
    weight = jnp.float32(0.0)
    for kind in range(weights_ref.shape[0]):
        weight = jnp.where(task_ref[0] == kind, weights_ref[kind], weight)
    line = lax.broadcasted_iota(jnp.int32, (8, HD), 0)
    note = jnp.where(line == 0, reward_ref[0, 0], length_ref[0, 0]).astype(F32)
    aux_ref[...] = jnp.where(line < 2, note, weight)
    for src, dst in ((rk_ref, rkt_ref), (rv_ref, rvt_ref)):
        dst[...] = jnp.transpose(src[...].astype(F32), (1, 0, 2)).astype(BF16)
    spread = lax.broadcasted_iota(jnp.int32, (toks, rows), 1) // QPK
    spread = (spread == lax.broadcasted_iota(jnp.int32, (toks, rows), 0)).astype(BF16)
    parts = []
    for h in range(HEADS):
        x = lse_ref[h] * LOG2E
        for _ in range(3):
            parts.append(x.astype(BF16))
            x = x - parts[-1].astype(F32)
    wide = dot(jnp.concatenate(parts, 0), spread, NN)
    line = lax.broadcasted_iota(jnp.int32, (QPK, rows), 0)
    lane = lax.broadcasted_iota(jnp.int32, (QPK, rows), 1)
    for h in range(HEADS):
        at = h * 3 * QPK
        x = wide[at : at + QPK] + (wide[at + QPK : at + 2 * QPK] + wide[at + 2 * QPK : at + 3 * QPK])
        x = jnp.sum(jnp.where(lane % QPK == line, x, 0.0), axis=0, keepdims=True)
        row_ref[h] = jnp.where(lane[0:1] // QPK < length_ref[0, 0], x, DEAD)


def resp_rows(reward, length, task, weights, wait, rk, rv, lse):
    toks = rk.shape[0]
    by_head = jax.ShapeDtypeStruct((HEADS, toks, HD), BF16)
    return pl.pallas_call(
        rows_body,
        in_specs=[pl.BlockSpec(memory_space=pltpu.SMEM)] * 4
        + [pl.BlockSpec(memory_space=pl.ANY)]
        + [WHOLE] * 3,
        out_specs=[WHOLE] * 4,
        out_shape=[
            by_head,
            by_head,
            jax.ShapeDtypeStruct((HEADS, 1, toks * QPK), F32),
            jax.ShapeDtypeStruct((8, HD), F32),
        ],
        compiler_params=pltpu.CompilerParams(vmem_limit_bytes=GRANT << 20),
        cost_estimate=cost(5 * 10**9, 1 << 20),
        name="rows",
    )(reward, length, task, weights, wait, rk, rv, lse)


def loop(body):
    lax.fori_loop(0, HEADS, lambda h, c: (body(h), c)[1], 0)


def resp_body(step, q_ref, go_ref, ao_ref, lse_ref, rk_ref, rv_ref, del_ref, ds_ref, dk_ref, dv_ref):
    toks = q_ref.shape[0]
    tb = step // QPK
    ones = jnp.ones((8, HD), BF16)

    def head(h):
        for i in reversed(range(toks // tb)):
            tok = pl.ds(i * tb, tb)
            cols = pl.ds(i * step, step)
            seen = (i + 1) * tb
            q = q_ref[tok, h].reshape(step, HD)
            go = go_ref[tok, h].reshape(step, HD)
            prod = go.astype(F32) * ao_ref[tok, h].reshape(step, HD).astype(F32)
            high = prod.astype(BF16)
            low = (prod - high.astype(F32)).astype(BF16)
            delta = (dot(ones, high, NT) + dot(ones, low, NT))[0:1]
            del_ref[h, :, cols] = delta
            k, v = rk_ref[h, :seen], rv_ref[h, :seen]
            s = dot(k, q, NT) * (SCALE * LOG2E) - lse_ref[h, :, cols]
            p = jnp.exp2(s)
            key = lax.broadcasted_iota(jnp.int32, (tb, step), 0)
            query = lax.broadcasted_iota(jnp.int32, (tb, step), 1) // QPK
            edge = jnp.where(key <= query, p[i * tb :], 0.0)
            p = jnp.concatenate([p[: i * tb], edge], 0) if i else edge
            ds = p * (dot(v, go, NT) - delta)
            pb, dsb = p.astype(BF16), ds.astype(BF16)
            ds_ref[h, :seen, cols] = dsb
            if seen < toks:
                ds_ref[h, seen:, cols] = jnp.zeros((toks - seen, step), BF16)
                dk_ref[h, :seen] += dot(dsb, q, NN)
                dv_ref[h, :seen] += dot(pb, go, NN)
            else:
                dk_ref[h] = dot(dsb, q, NN)
                dv_ref[h] = dot(pb, go, NN)

    loop(head)


def resp_grads(q, go, ao, lse, rk, rv):
    toks = q.shape[0]
    rows = toks * QPK
    return pl.pallas_call(
        functools.partial(resp_body, 1024),
        in_specs=[WHOLE] * 6,
        out_specs=[WHOLE] * 4,
        out_shape=[
            jax.ShapeDtypeStruct((HEADS, 1, rows), F32),
            jax.ShapeDtypeStruct((HEADS, toks, rows), BF16),
            jax.ShapeDtypeStruct((HEADS, toks, HD), F32),
            jax.ShapeDtypeStruct((HEADS, toks, HD), F32),
        ],
        compiler_params=pltpu.CompilerParams(vmem_limit_bytes=GRANT << 20),
        cost_estimate=cost(5 * 10**9, 1 << 20),
        name="resp",
    )(q, go, ao, lse, rk, rv)


def shard_keys(refs, h):
    k, v = [], []
    for r in refs:
        for at in range(0, r.shape[0], PAY):
            k.append(r[pl.ds(pl.multiple_of(at + h * SHARD, 16), SHARD)])
            v.append(r[pl.ds(pl.multiple_of(at + ROWS + h * SHARD, 16), SHARD)])
    return jnp.concatenate(k, 0), jnp.concatenate(v, 0)


def shard_rewards(refs):
    got = []
    for r in refs:
        for at in range(0, r.shape[0], PAY):
            tail = r[pl.ds(at + KV, 16)].astype(F32)
            got.append((tail[0:1] * 32.0 + tail[1:2], tail[2:3]))
    return got


def prompt_body(step, n, note, last, q_ref, go_ref, lse_ref, del_ref, stat_in, *refs):
    aux = refs[0] if last else None
    refs = refs[1:] if last else refs
    kv, ds_ref, outs, stat_ref = refs[:n], refs[n], refs[n + 1 : 2 * n + 1], refs[2 * n + 1]
    toks = q_ref.shape[0]
    tb = step // QPK
    got = shard_rewards(kv)
    total, square = stat_in[0:1], stat_in[1:2]
    for r, _ in got:
        total, square = total + r, square + r * r
    stat_ref[...] = stat_in[...]
    stat_ref[0:1], stat_ref[1:2] = total, square
    if note is not None:
        stat_ref[2:3], stat_ref[3:4] = got[note]
    factor = None
    if last:
        members = float(RING * PAIR)
        whole, pairs = total.astype(jnp.int32), square.astype(jnp.int32)
        spare = (RING * PAIR * pairs - whole * whole).astype(F32)
        spread = jnp.sqrt(jnp.maximum(spare, 0.0)) * (1.0 / (members * 256.0))
        weight = aux[2:3] / jnp.maximum(spread, 1.0)
        coefs = []
        for r, length in ((aux[0:1], aux[1:2]), (stat_in[2:3], stat_in[3:4])):
            coefs.append((r * members - total) * (1.0 / (members * 256.0)) * weight / length)
        stat_ref[0:1], stat_ref[1:2] = coefs
        factor = coefs[0]

    def head(h):
        k, v = shard_keys(kv, h)
        dk = dv = None
        for i in range(toks // tb):
            tok = pl.ds(i * tb, tb)
            cols = pl.ds(i * step, step)
            q = q_ref[tok, h].reshape(step, HD)
            go = go_ref[tok, h].reshape(step, HD)
            p = jnp.exp2(dot(k, q, NT) * (SCALE * LOG2E) - lse_ref[h, :, cols])
            ds = p * (dot(v, go, NT) - del_ref[h, :, cols])
            pb, dsb = p.astype(BF16), ds.astype(BF16)
            ds_ref[h, :, cols] = dsb
            a, b = dot(dsb, q, NN), dot(pb, go, NN)
            dk, dv = (a, b) if dk is None else (dk + a, dv + b)
        dk = dk * SCALE
        if last:
            dk, dv = dk * factor, dv * factor
        at = 0
        for out in outs:
            for y in range(PAIR):
                out[y, 0, h] = dk[at : at + SHARD].astype(BF16)
                out[y, 1, h] = dv[at : at + SHARD].astype(BF16)
                at += SHARD

    loop(head)


def prompt_grads(name, q, go, lse, delta, stat, aux, shards, note, last):
    rows = q.shape[0] * QPK
    keys = len(shards) * PAIR * SHARD
    extra = [aux] if last else []
    ins = [q, go, lse, delta, stat, *extra, *shards]
    pair = jax.ShapeDtypeStruct((PAIR, 2, HEADS, SHARD, HD), BF16)
    got = pl.pallas_call(
        functools.partial(prompt_body, 1024, len(shards), note, last),
        in_specs=[WHOLE] * len(ins),
        out_specs=[WHOLE] * (len(shards) + 2),
        out_shape=[
            jax.ShapeDtypeStruct((HEADS, keys, rows), BF16),
            *[pair] * len(shards),
            jax.ShapeDtypeStruct((8, HD), F32),
        ],
        compiler_params=pltpu.CompilerParams(vmem_limit_bytes=GRANT << 20),
        cost_estimate=cost((keys // 192) * 5 * 10**9 + 10**8, 1 << 20),
        name=name,
    )(*ins)
    return got[0], [x.reshape(PAIR * KV, HD) for x in got[1:-1]], got[-1]


def query_body(head, n_ds, counts, ins, coef_ref, *refs):
    ds, shards, rk_ref = refs[:n_ds], refs[n_ds : n_ds + sum(counts)], refs[n_ds + sum(counts)]
    out, coef_out, rows_ref, sems = refs[ins - 1 :]
    step = 512
    tb = step // QPK
    keys, at = [], 0
    for c in counts:
        keys.append(shard_keys(shards[at : at + c], head)[0])
        at += c
    keys.append(rk_ref[head])
    coef_out[...] = coef_ref[...]
    factor = coef_ref[0:1] * SCALE
    sends = []
    for i in range(ds[0].shape[2] // step):
        acc = None
        for d, k in zip(ds, keys):
            a = dot(k, d[head, :, pl.ds(i * step, step)], TN)
            acc = a if acc is None else acc + a
        rows_ref[i * tb : (i + 1) * tb] = (acc.T * factor).astype(BF16).reshape(tb, QPK, HD)
        tok = pl.ds(i * tb, tb)
        sends.append(pltpu.make_async_copy(rows_ref.at[tok], out.at[tok, head], sems.at[i]))
        sends[-1].start()
    for send in sends:
        send.wait()


def query_grads(head, coef, ds, groups, rk, so_far, *waits):
    toks = ds[0].shape[2] // QPK
    counts = [len(g) for g in groups]
    shards = [s for g in groups for s in g]
    there = pl.BlockSpec(memory_space=pl.ANY)
    ins = [coef, *ds, *shards, rk]
    specs = [WHOLE] * len(ins) + [there] * len(waits)
    ins += waits
    alias = {}
    if so_far is not None:
        alias = {len(ins): 0}
        ins.append(so_far)
        specs.append(there)
    return pl.pallas_call(
        functools.partial(query_body, head, len(ds), counts, len(ins)),
        in_specs=specs,
        out_specs=[there, WHOLE],
        out_shape=[
            jax.ShapeDtypeStruct((toks, HEADS, QPK, HD), BF16),
            jax.ShapeDtypeStruct((8, HD), F32),
        ],
        input_output_aliases=alias,
        scratch_shapes=[pltpu.VMEM((toks, QPK, HD), BF16), pltpu.SemaphoreType.DMA((4,))],
        compiler_params=pltpu.CompilerParams(vmem_limit_bytes=GRANT << 20),
        cost_estimate=cost(4 * 10**9, 1 << 20),
        name="dq",
    )(*ins)


def out_body(coef_ref, dk_ref, dv_ref, drk_ref, drv_ref, coef_out):
    coef_out[...] = coef_ref[...]
    factor = coef_ref[0:1]
    for src, dst, c in ((dk_ref, drk_ref, factor * SCALE), (dv_ref, drv_ref, factor)):
        dst[...] = jnp.transpose(src[...] * c, (1, 0, 2)).astype(BF16)


def resp_out(coef, dk, dv):
    out = jax.ShapeDtypeStruct((dk.shape[1], HEADS, HD), BF16)
    return pl.pallas_call(
        out_body,
        in_specs=[WHOLE] * 3,
        out_specs=[WHOLE] * 3,
        out_shape=[out, out, jax.ShapeDtypeStruct((8, HD), F32)],
        compiler_params=pltpu.CompilerParams(vmem_limit_bytes=GRANT << 20),
        cost_estimate=cost(4 * 10**9, 1 << 20),
        name="out",
    )(coef, dk, dv)


def hop(x, dz, dy=0):
    pairs = [
        (z * PAIR + y, ((z + dz) % RING) * PAIR + (y + dy) % PAIR)
        for z in range(RING)
        for y in range(PAIR)
    ]
    return lax.ppermute(x, "group", pairs)


def swap_core(x):
    return lax.ppermute(x, "tensor", [(0, 1), (1, 0)])


def in_order(core, mine, other, axis):
    return jnp.where(
        core == 0,
        jnp.concatenate([mine, other], axis),
        jnp.concatenate([other, mine], axis),
    )


def on_device(
    queries,
    resp_keys,
    resp_values,
    prompt_keys,
    prompt_values,
    attn_out,
    grad_out,
    log_sums,
    prompt_lengths,
    resp_lengths,
    rewards,
    task_ids,
    task_weights,
):
    core = lax.axis_index("tensor")
    member = lax.axis_index("group")
    toks = queries.shape[2]
    part = prompt_keys.shape[1]
    length = resp_lengths[0, 0]
    reward = rewards[0, 0]

    mine, theirs = split_heads(prompt_lengths, prompt_keys, prompt_values)
    own = join_tokens(rewards, resp_lengths, mine, swap_core(theirs))

    q, go, ao = queries[0, 0], grad_out[0, 0], attn_out[0, 0]
    rk, rv, lse, aux = resp_rows(
        rewards,
        resp_lengths,
        task_ids,
        task_weights,
        own,
        resp_keys[0, 0],
        resp_values[0, 0],
        log_sums[0, 0],
    )
    stat = jnp.zeros((8, HD), F32)

    delta, ds_r, dk_r, dv_r = resp_grads(q, go, ao, lse, rk, rv)
    pair = join_pair(lse, own, hop(own, 0, 1))
    back1, fore1 = hop(pair, 1), hop(pair, -1)
    far = hop(pair, 4)
    back2, fore2 = hop(back1, 1), hop(fore1, -1)
    back3, fore3 = hop(back2, 1), hop(fore2, -1)

    common = (q, go, lse, delta)
    ds_1, (here, down_1, up_1, across), stat = prompt_grads(
        "near", *common, stat, None, [pair, back1, fore1, far], 3 * PAIR, False
    )
    ds_2, (down_2, up_2), stat = prompt_grads(
        "second", *common, stat, None, [back2, fore2], None, False
    )
    ds_3, (down_3, up_3), coef = prompt_grads(
        "third", *common, stat, aux, [back3, fore3], None, True
    )

    groups = [[pair, back1, fore1, far], [back2, fore2], [back3, fore3]]
    ds_all = [ds_1, ds_2, ds_3, ds_r]

    def dq(head, so_far, *waits):
        return query_grads(head, coef, ds_all, groups, rk, so_far, *waits)

    def add(a, c, b):
        return (a.astype(F32) + c[0:1] * b.astype(F32)).astype(BF16)

    down, up = hop(down_3, -1), hop(up_3, 1)
    grad_q, _ = dq(0, None)
    grad_q, _ = dq(1, grad_q)
    grad_q, again = dq(2, grad_q)
    down, up = add(down, again, down_2), add(up, again, up_2)
    far_term = hop(across, 4)
    grad_q, again = dq(3, grad_q, down, up)
    drk, drv, again = resp_out(again, dk_r, dv_r)
    down, up = hop(down, -1), hop(up, 1)
    down, up = add(down, again, down_1), add(up, again, up_1)
    down, up = hop(down, -1), hop(up, 1)
    home = coef[0:1] * here.astype(F32) + coef[1:2] * far_term.astype(F32)
    home = home + down.astype(F32) + up.astype(F32)
    beside = hop(home[KV:].astype(BF16), 0, 1)
    home = (home[:KV] + beside.astype(F32)).reshape(2, HEADS, 2, part, HD)
    keep = lax.dynamic_index_in_dim(home, core, 2, keepdims=False)
    give = lax.dynamic_index_in_dim(home, 1 - core, 2, keepdims=False)
    take = swap_core(give)
    done = in_order(core, keep, take, 1).transpose(0, 2, 1, 3).astype(BF16)
    slot = (member * 2 + core) * part + jnp.arange(part)
    done = jnp.where((slot < prompt_lengths[0])[None, :, None, None], done, 0)
    return (
        grad_q.reshape(1, 1, toks, HEADS, QPK, HD),
        drk[None, None],
        drv[None, None],
        done[0][None],
        done[1][None],
    )


def solution(mesh):
    wide = P("prompt", "group", None, "tensor", None, None)
    resp = P("prompt", "group", None, "tensor", None)
    prompt = P("prompt", ("group", "tensor"), None, None)
    return jax.shard_map(
        on_device,
        mesh=mesh,
        in_specs=(
            wide,
            resp,
            resp,
            prompt,
            prompt,
            wide,
            wide,
            P("prompt", "group", "tensor", None, None),
            P("prompt"),
            P("prompt", "group"),
            P("prompt", "group"),
            P("prompt"),
            P(),
        ),
        out_specs=(wide, resp, resp, prompt, prompt),
        check_vma=False,
    )
```

```python
import functools
import math

import jax
import jax.numpy as jnp
from jax import lax
from jax.experimental import pallas as pl
from jax.experimental.pallas import tpu as pltpu
from jax.sharding import PartitionSpec as P

HEADS = 4
QPK = 8
HD = 128
SHARD = 48
ROWS = HEADS * SHARD
KV = 2 * ROWS
PAY = KV + 16
RING = 8
PAIR = 2
SCALE = HD ** (-0.5)
LOG2E = math.log2(math.e)
DEAD = 1e30
WHOLE = pl.BlockSpec(memory_space=pltpu.VMEM)
GRANT = 20
SMALL = 4
NT = (((1,), (1,)), ((), ()))
NN = (((1,), (0,)), ((), ()))
TN = (((0,), (0,)), ((), ()))
F32, BF16 = jnp.float32, jnp.bfloat16


def dot(a, b, dims):
    return lax.dot_general(a, b, dims, preferred_element_type=F32)


def cost(flops, traffic):
    return pl.CostEstimate(flops=flops, bytes_accessed=traffic, transcendentals=0)


def split_body(live_ref, pk_ref, pv_ref, mine_ref, theirs_ref):
    core, member = lax.axis_index("tensor"), lax.axis_index("group")
    part = pk_ref.shape[1]
    slot = (member * 2 + core) * part + lax.broadcasted_iota(jnp.int32, pk_ref.shape[1:], 0)
    keys = jnp.where(slot < live_ref[0], pk_ref[0].astype(F32), 0.0)
    for at, x in enumerate((keys, pv_ref[0].astype(F32))):
        x = jnp.transpose(x, (1, 0, 2))
        low, high = x[:HEADS], x[HEADS:]
        mine_ref[at] = jnp.where(core == 0, low, high)
        theirs_ref[at] = jnp.where(core == 0, high, low)


def split_heads(live, pk, pv):
    part = pk.shape[1]
    whole = pl.BlockSpec(memory_space=pltpu.VMEM)
    half = jax.ShapeDtypeStruct((2, HEADS, part, HD), F32)
    return pl.pallas_call(
        split_body,
        in_specs=[pl.BlockSpec(memory_space=pltpu.SMEM), whole, whole],
        out_specs=[whole, whole],
        out_shape=[half, half],
        compiler_params=pltpu.CompilerParams(vmem_limit_bytes=SMALL << 20),
        name="split",
    )(live, pk, pv)


def join_body(reward_ref, mine_ref, got_ref, out_ref):
    core = lax.axis_index("tensor")
    for at in range(2):
        for h in range(HEADS):
            a, b = mine_ref[at, h], got_ref[at, h]
            pair = [jnp.where(core == 0, a, b), jnp.where(core == 0, b, a)]
            first = (at * HEADS + h) * SHARD
            out_ref[first : first + SHARD] = jnp.concatenate(pair, 0).astype(BF16)
    reward = reward_ref[0, 0]
    line = lax.broadcasted_iota(jnp.int32, (16, HD), 0)
    note = jnp.where(line == 0, reward >> 5, reward & 31)
    out_ref[KV:] = note.astype(F32).astype(BF16)


def join_tokens(reward, mine, got):
    whole = pl.BlockSpec(memory_space=pltpu.VMEM)
    number = pl.BlockSpec(memory_space=pltpu.SMEM)
    return pl.pallas_call(
        join_body,
        in_specs=[number] + [whole] * 2,
        out_specs=whole,
        out_shape=jax.ShapeDtypeStruct((PAY, HD), BF16),
        compiler_params=pltpu.CompilerParams(vmem_limit_bytes=SMALL << 20),
        name="join",
    )(reward, mine, got)


def pair_body(wait_ref, own_ref, beside_ref, out_ref):
    out_ref[:PAY] = own_ref[...]
    out_ref[PAY:] = beside_ref[...]


def join_pair(wait, own, beside):
    return pl.pallas_call(
        pair_body,
        in_specs=[pl.BlockSpec(memory_space=pl.ANY), WHOLE, WHOLE],
        out_specs=WHOLE,
        out_shape=jax.ShapeDtypeStruct((PAIR * PAY, HD), BF16),
        compiler_params=pltpu.CompilerParams(vmem_limit_bytes=SMALL << 20),
        name="pair",
    )(wait, own, beside)


def rows_body(reward_ref, length_ref, task_ref, weights_ref, wait_ref, rk_ref, rv_ref, lse_ref, *refs):
    rkt_ref, rvt_ref, row_ref, aux_ref = refs
    toks = rk_ref.shape[0]
    rows = toks * QPK
    weight = jnp.float32(0.0)
    for kind in range(weights_ref.shape[0]):
        weight = jnp.where(task_ref[0] == kind, weights_ref[kind], weight)
    line = lax.broadcasted_iota(jnp.int32, (8, HD), 0)
    note = jnp.where(line == 0, reward_ref[0, 0], length_ref[0, 0]).astype(F32)
    aux_ref[...] = jnp.where(line < 2, note, weight)
    for src, dst in ((rk_ref, rkt_ref), (rv_ref, rvt_ref)):
        dst[...] = jnp.transpose(src[...].astype(F32), (1, 0, 2)).astype(BF16)
    spread = lax.broadcasted_iota(jnp.int32, (toks, rows), 1) // QPK
    spread = (spread == lax.broadcasted_iota(jnp.int32, (toks, rows), 0)).astype(BF16)
    parts = []
    for h in range(HEADS):
        x = lse_ref[h] * LOG2E
        for _ in range(3):
            parts.append(x.astype(BF16))
            x = x - parts[-1].astype(F32)
    wide = dot(jnp.concatenate(parts, 0), spread, NN)
    line = lax.broadcasted_iota(jnp.int32, (QPK, rows), 0)
    lane = lax.broadcasted_iota(jnp.int32, (QPK, rows), 1)
    for h in range(HEADS):
        at = h * 3 * QPK
        x = wide[at : at + QPK] + (wide[at + QPK : at + 2 * QPK] + wide[at + 2 * QPK : at + 3 * QPK])
        x = jnp.sum(jnp.where(lane % QPK == line, x, 0.0), axis=0, keepdims=True)
        row_ref[h] = jnp.where(lane[0:1] // QPK < length_ref[0, 0], x, DEAD)


def resp_rows(reward, length, task, weights, wait, rk, rv, lse):
    toks = rk.shape[0]
    by_head = jax.ShapeDtypeStruct((HEADS, toks, HD), BF16)
    return pl.pallas_call(
        rows_body,
        in_specs=[pl.BlockSpec(memory_space=pltpu.SMEM)] * 4
        + [pl.BlockSpec(memory_space=pl.ANY)]
        + [WHOLE] * 3,
        out_specs=[WHOLE] * 4,
        out_shape=[
            by_head,
            by_head,
            jax.ShapeDtypeStruct((HEADS, 1, toks * QPK), F32),
            jax.ShapeDtypeStruct((8, HD), F32),
        ],
        compiler_params=pltpu.CompilerParams(vmem_limit_bytes=GRANT << 20),
        cost_estimate=cost(5 * 10**9, 1 << 20),
        name="rows",
    )(reward, length, task, weights, wait, rk, rv, lse)


def loop(body):
    lax.fori_loop(0, HEADS, lambda h, c: (body(h), c)[1], 0)


def resp_body(step, q_ref, go_ref, ao_ref, lse_ref, rk_ref, rv_ref, del_ref, ds_ref, dk_ref, dv_ref):
    toks = q_ref.shape[0]
    tb = step // QPK
    ones = jnp.ones((8, HD), BF16)

    def head(h):
        for i in reversed(range(toks // tb)):
            tok = pl.ds(i * tb, tb)
            cols = pl.ds(i * step, step)
            seen = (i + 1) * tb
            q = q_ref[tok, h].reshape(step, HD)
            go = go_ref[tok, h].reshape(step, HD)
            prod = go.astype(F32) * ao_ref[tok, h].reshape(step, HD).astype(F32)
            high = prod.astype(BF16)
            low = (prod - high.astype(F32)).astype(BF16)
            delta = (dot(ones, high, NT) + dot(ones, low, NT))[0:1]
            del_ref[h, :, cols] = delta
            k, v = rk_ref[h, :seen], rv_ref[h, :seen]
            s = dot(k, q, NT) * (SCALE * LOG2E) - lse_ref[h, :, cols]
            p = jnp.exp2(s)
            key = lax.broadcasted_iota(jnp.int32, (tb, step), 0)
            query = lax.broadcasted_iota(jnp.int32, (tb, step), 1) // QPK
            edge = jnp.where(key <= query, p[i * tb :], 0.0)
            p = jnp.concatenate([p[: i * tb], edge], 0) if i else edge
            ds = p * (dot(v, go, NT) - delta)
            pb, dsb = p.astype(BF16), ds.astype(BF16)
            ds_ref[h, :seen, cols] = dsb
            if seen < toks:
                ds_ref[h, seen:, cols] = jnp.zeros((toks - seen, step), BF16)
                dk_ref[h, :seen] += dot(dsb, q, NN)
                dv_ref[h, :seen] += dot(pb, go, NN)
            else:
                dk_ref[h] = dot(dsb, q, NN)
                dv_ref[h] = dot(pb, go, NN)

    loop(head)


def resp_grads(q, go, ao, lse, rk, rv):
    toks = q.shape[0]
    rows = toks * QPK
    return pl.pallas_call(
        functools.partial(resp_body, 1024),
        in_specs=[WHOLE] * 6,
        out_specs=[WHOLE] * 4,
        out_shape=[
            jax.ShapeDtypeStruct((HEADS, 1, rows), F32),
            jax.ShapeDtypeStruct((HEADS, toks, rows), BF16),
            jax.ShapeDtypeStruct((HEADS, toks, HD), F32),
            jax.ShapeDtypeStruct((HEADS, toks, HD), F32),
        ],
        compiler_params=pltpu.CompilerParams(vmem_limit_bytes=GRANT << 20),
        cost_estimate=cost(5 * 10**9, 1 << 20),
        name="resp",
    )(q, go, ao, lse, rk, rv)


def shard_keys(refs, h):
    k, v = [], []
    for r in refs:
        for at in range(0, r.shape[0], PAY):
            k.append(r[pl.ds(pl.multiple_of(at + h * SHARD, 16), SHARD)])
            v.append(r[pl.ds(pl.multiple_of(at + ROWS + h * SHARD, 16), SHARD)])
    return jnp.concatenate(k, 0), jnp.concatenate(v, 0)


def shard_rewards(refs):
    got = []
    for r in refs:
        for at in range(0, r.shape[0], PAY):
            tail = r[pl.ds(at + KV, 16)].astype(F32)
            got.append(tail[0:1] * 32.0 + tail[1:2])
    return got


def prompt_body(step, n, waits, last, q_ref, go_ref, lse_ref, del_ref, stat_in, *refs):
    aux = refs[0] if last else None
    refs = refs[1:] if last else refs
    kv, refs = refs[:n], refs[n + waits :]
    ds_ref, outs, stat_ref = refs[0], refs[1 : n + 1], refs[n + 1]
    toks = q_ref.shape[0]
    tb = step // QPK
    got = shard_rewards(kv)
    total, square = stat_in[0:1], stat_in[1:2]
    for r in got:
        total, square = total + r, square + r * r
    stat_ref[...] = stat_in[...]
    stat_ref[0:1], stat_ref[1:2] = total, square
    factor = None
    if last:
        members = float(RING * PAIR)
        whole, pairs = total.astype(jnp.int32), square.astype(jnp.int32)
        spare = (RING * PAIR * pairs - whole * whole).astype(F32)
        spread = jnp.sqrt(jnp.maximum(spare, 0.0)) * (1.0 / (members * 256.0))
        weight = aux[2:3] / jnp.maximum(spread, 1.0)
        score = (aux[0:1] * members - total) * (1.0 / (members * 256.0))
        factor = score * weight / aux[1:2]
        stat_ref[0:1] = factor

    def head(h):
        k, v = shard_keys(kv, h)
        dk = dv = None
        for i in range(toks // tb):
            tok = pl.ds(i * tb, tb)
            cols = pl.ds(i * step, step)
            q = q_ref[tok, h].reshape(step, HD)
            go = go_ref[tok, h].reshape(step, HD)
            p = jnp.exp2(dot(k, q, NT) * (SCALE * LOG2E) - lse_ref[h, :, cols])
            ds = p * (dot(v, go, NT) - del_ref[h, :, cols])
            pb, dsb = p.astype(BF16), ds.astype(BF16)
            ds_ref[h, :, cols] = dsb
            a, b = dot(dsb, q, NN), dot(pb, go, NN)
            dk, dv = (a, b) if dk is None else (dk + a, dv + b)
        dk = dk * SCALE
        if last:
            dk, dv = dk * factor, dv * factor
        at = 0
        for out in outs:
            for y in range(PAIR):
                out[y, 0, h] = dk[at : at + SHARD].astype(BF16)
                out[y, 1, h] = dv[at : at + SHARD].astype(BF16)
                at += SHARD

    loop(head)


def prompt_grads(name, q, go, lse, delta, stat, aux, shards, last, *waits):
    rows = q.shape[0] * QPK
    keys = len(shards) * PAIR * SHARD
    extra = [aux] if last else []
    ins = [q, go, lse, delta, stat, *extra, *shards]
    pair = jax.ShapeDtypeStruct((PAIR, 2, HEADS, SHARD, HD), BF16)
    got = pl.pallas_call(
        functools.partial(prompt_body, 1024, len(shards), len(waits), last),
        in_specs=[WHOLE] * len(ins) + [pl.BlockSpec(memory_space=pl.ANY)] * len(waits),
        out_specs=[WHOLE] * (len(shards) + 2),
        out_shape=[
            jax.ShapeDtypeStruct((HEADS, keys, rows), BF16),
            *[pair] * len(shards),
            jax.ShapeDtypeStruct((8, HD), F32),
        ],
        compiler_params=pltpu.CompilerParams(vmem_limit_bytes=GRANT << 20),
        cost_estimate=cost((keys // 192) * 5 * 10**9 + 10**8, 1 << 20),
        name=name,
    )(*ins, *waits)
    return got[0], [x.reshape(PAIR * KV, HD) for x in got[1:-1]], got[-1]


def query_body(head, n_ds, counts, carry, ins, coef_ref, *refs):
    ds, shards, rk_ref = refs[:n_ds], refs[n_ds : n_ds + sum(counts)], refs[n_ds + sum(counts)]
    out, coef_out, rows_ref, sems = refs[ins - 1 : ins + 1] + refs[-2:]
    if carry:
        sums = refs[n_ds + sum(counts) + 1][...].astype(F32)
        refs[ins + 1][...] = (sums * coef_ref[0:1]).astype(BF16)
    step = 512
    tb = step // QPK
    keys, at = [], 0
    for c in counts:
        keys.append(shard_keys(shards[at : at + c], head)[0])
        at += c
    keys.append(rk_ref[head])
    coef_out[...] = coef_ref[...]
    factor = coef_ref[0:1] * SCALE
    sends = []
    for i in range(ds[0].shape[2] // step):
        acc = None
        for d, k in zip(ds, keys):
            a = dot(k, d[head, :, pl.ds(i * step, step)], TN)
            acc = a if acc is None else acc + a
        rows_ref[i * tb : (i + 1) * tb] = (acc.T * factor).astype(BF16).reshape(tb, QPK, HD)
        tok = pl.ds(i * tb, tb)
        sends.append(pltpu.make_async_copy(rows_ref.at[tok], out.at[tok, head], sems.at[i]))
        sends[-1].start()
    for send in sends:
        send.wait()


def query_grads(head, coef, ds, groups, rk, so_far, carry, *waits):
    toks = ds[0].shape[2] // QPK
    counts = [len(g) for g in groups]
    shards = [s for g in groups for s in g]
    there = pl.BlockSpec(memory_space=pl.ANY)
    ins = [coef, *ds, *shards, rk] + ([] if carry is None else [carry])
    more = [] if carry is None else [jax.ShapeDtypeStruct(carry.shape, BF16)]
    specs = [WHOLE] * len(ins) + [there] * len(waits)
    ins += waits
    alias = {}
    if so_far is not None:
        alias = {len(ins): 0}
        ins.append(so_far)
        specs.append(there)
    return pl.pallas_call(
        functools.partial(query_body, head, len(ds), counts, carry is not None, len(ins)),
        in_specs=specs,
        out_specs=[there, WHOLE] + [WHOLE] * len(more),
        out_shape=[
            jax.ShapeDtypeStruct((toks, HEADS, QPK, HD), BF16),
            jax.ShapeDtypeStruct((8, HD), F32),
            *more,
        ],
        input_output_aliases=alias,
        scratch_shapes=[pltpu.VMEM((toks, QPK, HD), BF16), pltpu.SemaphoreType.DMA((4,))],
        compiler_params=pltpu.CompilerParams(vmem_limit_bytes=GRANT << 20),
        cost_estimate=cost(4 * 10**9, 1 << 20),
        name="dq",
    )(*ins)


def out_body(coef_ref, dk_ref, dv_ref, drk_ref, drv_ref, coef_out):
    coef_out[...] = coef_ref[...]
    factor = coef_ref[0:1]
    for src, dst, c in ((dk_ref, drk_ref, factor * SCALE), (dv_ref, drv_ref, factor)):
        dst[...] = jnp.transpose(src[...] * c, (1, 0, 2)).astype(BF16)


def resp_out(coef, dk, dv):
    out = jax.ShapeDtypeStruct((dk.shape[1], HEADS, HD), BF16)
    return pl.pallas_call(
        out_body,
        in_specs=[WHOLE] * 3,
        out_specs=[WHOLE] * 3,
        out_shape=[out, out, jax.ShapeDtypeStruct((8, HD), F32)],
        compiler_params=pltpu.CompilerParams(vmem_limit_bytes=GRANT << 20),
        cost_estimate=cost(4 * 10**9, 1 << 20),
        name="out",
    )(coef, dk, dv)


def hop(x, dz, dy=0):
    pairs = [
        (z * PAIR + y, ((z + dz) % RING) * PAIR + (y + dy) % PAIR)
        for z in range(RING)
        for y in range(PAIR)
    ]
    return lax.ppermute(x, "group", pairs)


def swap_core(x):
    return lax.ppermute(x, "tensor", [(0, 1), (1, 0)])


def in_order(core, mine, other, axis):
    return jnp.where(
        core == 0,
        jnp.concatenate([mine, other], axis),
        jnp.concatenate([other, mine], axis),
    )


def on_device(
    queries,
    resp_keys,
    resp_values,
    prompt_keys,
    prompt_values,
    attn_out,
    grad_out,
    log_sums,
    prompt_lengths,
    resp_lengths,
    rewards,
    task_ids,
    task_weights,
):
    core = lax.axis_index("tensor")
    member = lax.axis_index("group")
    toks = queries.shape[2]
    part = prompt_keys.shape[1]
    length = resp_lengths[0, 0]
    reward = rewards[0, 0]

    mine, theirs = split_heads(prompt_lengths, prompt_keys, prompt_values)
    own = join_tokens(rewards, mine, swap_core(theirs))

    q, go, ao = queries[0, 0], grad_out[0, 0], attn_out[0, 0]
    rk, rv, lse, aux = resp_rows(
        rewards,
        resp_lengths,
        task_ids,
        task_weights,
        own,
        resp_keys[0, 0],
        resp_values[0, 0],
        log_sums[0, 0],
    )
    stat = jnp.zeros((8, HD), F32)

    delta, ds_r, dk_r, dv_r = resp_grads(q, go, ao, lse, rk, rv)
    pair = join_pair(lse, own, hop(own, 0, 1))
    back1, fore1 = hop(pair, 1), hop(pair, -1)
    far = hop(pair, 4)
    back2, fore2 = hop(back1, 1), hop(fore1, -1)
    back3, fore3 = hop(back2, 1), hop(fore2, -1)

    common = (q, go, lse, delta)
    ds_1, (here, down_1, up_1), stat = prompt_grads(
        "near", *common, stat, None, [pair, back1, fore1], False, far
    )
    ds_2, (down_2, up_2, across), stat = prompt_grads(
        "second", *common, stat, None, [back2, fore2, far], False
    )
    ds_3, (down_3, up_3), coef = prompt_grads(
        "third", *common, stat, aux, [back3, fore3], True
    )

    groups = [[pair, back1, fore1], [back2, fore2, far], [back3, fore3]]
    ds_all = [ds_1, ds_2, ds_3, ds_r]

    def dq(head, so_far, carry, *waits):
        return query_grads(head, coef, ds_all, groups, rk, so_far, carry, *waits)

    def add(a, c, b):
        return (a.astype(F32) + c[0:1] * b.astype(F32)).astype(BF16)

    down, up = hop(down_3, -1), hop(up_3, 1)
    grad_q, _, across = dq(0, None, across)
    far_term = hop(across, 4)
    grad_q, again = dq(1, grad_q, None)
    down, up = add(down, again, down_2), add(up, again, up_2)
    grad_q, again = dq(2, grad_q, None, down, up)
    drk, drv, again = resp_out(again, dk_r, dv_r)
    down, up = hop(down, -1), hop(up, 1)
    down, up = add(down, again, down_1), add(up, again, up_1)
    grad_q, again = dq(3, grad_q, None, down, up)
    down, up = hop(down, -1), hop(up, 1)
    home = again[0:1] * here.astype(F32) + far_term.astype(F32)
    home = home + down.astype(F32) + up.astype(F32)
    beside = hop(home[KV:].astype(BF16), 0, 1)
    home = (home[:KV] + beside.astype(F32)).reshape(2, HEADS, 2, part, HD)
    keep = lax.dynamic_index_in_dim(home, core, 2, keepdims=False)
    give = lax.dynamic_index_in_dim(home, 1 - core, 2, keepdims=False)
    take = swap_core(give)
    done = in_order(core, keep, take, 1).transpose(0, 2, 1, 3).astype(BF16)
    slot = (member * 2 + core) * part + jnp.arange(part)
    done = jnp.where((slot < prompt_lengths[0])[None, :, None, None], done, 0)
    return (
        grad_q.reshape(1, 1, toks, HEADS, QPK, HD),
        drk[None, None],
        drv[None, None],
        done[0][None],
        done[1][None],
    )


def solution(mesh):
    wide = P("prompt", "group", None, "tensor", None, None)
    resp = P("prompt", "group", None, "tensor", None)
    prompt = P("prompt", ("group", "tensor"), None, None)
    return jax.shard_map(
        on_device,
        mesh=mesh,
        in_specs=(
            wide,
            resp,
            resp,
            prompt,
            prompt,
            wide,
            wide,
            P("prompt", "group", "tensor", None, None),
            P("prompt"),
            P("prompt", "group"),
            P("prompt", "group"),
            P("prompt"),
            P(),
        ),
        out_specs=(wide, resp, resp, prompt, prompt),
        check_vma=False,
    )
```

```python
import functools
import math

import jax
import jax.numpy as jnp
from jax import lax
from jax.experimental import pallas as pl
from jax.experimental.pallas import tpu as pltpu
from jax.sharding import PartitionSpec as P

HEADS = 4
QPK = 8
HD = 128
SHARD = 48
ROWS = HEADS * SHARD
KV = 2 * ROWS
PAY = KV + 16
RING = 8
PAIR = 2
SCALE = HD ** (-0.5)
LOG2E = math.log2(math.e)
DEAD = 1e30
WHOLE = pl.BlockSpec(memory_space=pltpu.VMEM)
GRANT = 20
SMALL = 4
NT = (((1,), (1,)), ((), ()))
NN = (((1,), (0,)), ((), ()))
TN = (((0,), (0,)), ((), ()))
F32, BF16 = jnp.float32, jnp.bfloat16


def dot(a, b, dims):
    return lax.dot_general(a, b, dims, preferred_element_type=F32)


def cost(flops, traffic):
    return pl.CostEstimate(flops=flops, bytes_accessed=traffic, transcendentals=0)


def split_body(live_ref, pk_ref, pv_ref, mine_ref, theirs_ref):
    core, member = lax.axis_index("tensor"), lax.axis_index("group")
    part = pk_ref.shape[1]
    slot = (member * 2 + core) * part + lax.broadcasted_iota(jnp.int32, pk_ref.shape[1:], 0)
    keys = jnp.where(slot < live_ref[0], pk_ref[0].astype(F32), 0.0)
    for at, x in enumerate((keys, pv_ref[0].astype(F32))):
        x = jnp.transpose(x, (1, 0, 2))
        low, high = x[:HEADS], x[HEADS:]
        mine_ref[at] = jnp.where(core == 0, low, high)
        theirs_ref[at] = jnp.where(core == 0, high, low)


def split_heads(live, pk, pv):
    part = pk.shape[1]
    whole = pl.BlockSpec(memory_space=pltpu.VMEM)
    half = jax.ShapeDtypeStruct((2, HEADS, part, HD), F32)
    return pl.pallas_call(
        split_body,
        in_specs=[pl.BlockSpec(memory_space=pltpu.SMEM), whole, whole],
        out_specs=[whole, whole],
        out_shape=[half, half],
        compiler_params=pltpu.CompilerParams(vmem_limit_bytes=SMALL << 20),
        name="split",
    )(live, pk, pv)


def join_body(reward_ref, length_ref, mine_ref, got_ref, out_ref):
    core = lax.axis_index("tensor")
    for at in range(2):
        for h in range(HEADS):
            a, b = mine_ref[at, h], got_ref[at, h]
            pair = [jnp.where(core == 0, a, b), jnp.where(core == 0, b, a)]
            first = (at * HEADS + h) * SHARD
            out_ref[first : first + SHARD] = jnp.concatenate(pair, 0).astype(BF16)
    reward, length = reward_ref[0, 0], length_ref[0, 0]
    line = lax.broadcasted_iota(jnp.int32, (16, HD), 0)
    note = jnp.where(line == 0, reward >> 5, jnp.where(line == 1, reward & 31, length))
    out_ref[KV:] = note.astype(F32).astype(BF16)


def join_tokens(reward, length, mine, got):
    whole = pl.BlockSpec(memory_space=pltpu.VMEM)
    number = pl.BlockSpec(memory_space=pltpu.SMEM)
    return pl.pallas_call(
        join_body,
        in_specs=[number] * 2 + [whole] * 2,
        out_specs=whole,
        out_shape=jax.ShapeDtypeStruct((PAY, HD), BF16),
        compiler_params=pltpu.CompilerParams(vmem_limit_bytes=SMALL << 20),
        name="join",
    )(reward, length, mine, got)


def pair_body(wait_ref, own_ref, beside_ref, out_ref):
    out_ref[:PAY] = own_ref[...]
    out_ref[PAY:] = beside_ref[...]


def join_pair(wait, own, beside):
    return pl.pallas_call(
        pair_body,
        in_specs=[pl.BlockSpec(memory_space=pl.ANY), WHOLE, WHOLE],
        out_specs=WHOLE,
        out_shape=jax.ShapeDtypeStruct((PAIR * PAY, HD), BF16),
        compiler_params=pltpu.CompilerParams(vmem_limit_bytes=SMALL << 20),
        name="pair",
    )(wait, own, beside)


def rows_body(reward_ref, length_ref, task_ref, weights_ref, wait_ref, rk_ref, rv_ref, lse_ref, *refs):
    rkt_ref, rvt_ref, row_ref, aux_ref = refs
    toks = rk_ref.shape[0]
    rows = toks * QPK
    weight = jnp.float32(0.0)
    for kind in range(weights_ref.shape[0]):
        weight = jnp.where(task_ref[0] == kind, weights_ref[kind], weight)
    line = lax.broadcasted_iota(jnp.int32, (8, HD), 0)
    note = jnp.where(line == 0, reward_ref[0, 0], length_ref[0, 0]).astype(F32)
    aux_ref[...] = jnp.where(line < 2, note, weight)
    for src, dst in ((rk_ref, rkt_ref), (rv_ref, rvt_ref)):
        dst[...] = jnp.transpose(src[...].astype(F32), (1, 0, 2)).astype(BF16)
    spread = lax.broadcasted_iota(jnp.int32, (toks, rows), 1) // QPK
    spread = (spread == lax.broadcasted_iota(jnp.int32, (toks, rows), 0)).astype(BF16)
    parts = []
    for h in range(HEADS):
        x = lse_ref[h] * LOG2E
        for _ in range(3):
            parts.append(x.astype(BF16))
            x = x - parts[-1].astype(F32)
    wide = dot(jnp.concatenate(parts, 0), spread, NN)
    line = lax.broadcasted_iota(jnp.int32, (QPK, rows), 0)
    lane = lax.broadcasted_iota(jnp.int32, (QPK, rows), 1)
    for h in range(HEADS):
        at = h * 3 * QPK
        x = wide[at : at + QPK] + (wide[at + QPK : at + 2 * QPK] + wide[at + 2 * QPK : at + 3 * QPK])
        x = jnp.sum(jnp.where(lane % QPK == line, x, 0.0), axis=0, keepdims=True)
        row_ref[h] = jnp.where(lane[0:1] // QPK < length_ref[0, 0], x, DEAD)


def resp_rows(reward, length, task, weights, wait, rk, rv, lse):
    toks = rk.shape[0]
    by_head = jax.ShapeDtypeStruct((HEADS, toks, HD), BF16)
    return pl.pallas_call(
        rows_body,
        in_specs=[pl.BlockSpec(memory_space=pltpu.SMEM)] * 4
        + [pl.BlockSpec(memory_space=pl.ANY)]
        + [WHOLE] * 3,
        out_specs=[WHOLE] * 4,
        out_shape=[
            by_head,
            by_head,
            jax.ShapeDtypeStruct((HEADS, 1, toks * QPK), F32),
            jax.ShapeDtypeStruct((8, HD), F32),
        ],
        compiler_params=pltpu.CompilerParams(vmem_limit_bytes=GRANT << 20),
        cost_estimate=cost(5 * 10**9, 1 << 20),
        name="rows",
    )(reward, length, task, weights, wait, rk, rv, lse)


def loop(body):
    lax.fori_loop(0, HEADS, lambda h, c: (body(h), c)[1], 0)


def resp_body(step, q_ref, go_ref, ao_ref, lse_ref, rk_ref, rv_ref, del_ref, ds_ref, dk_ref, dv_ref):
    toks = q_ref.shape[0]
    tb = step // QPK
    ones = jnp.ones((8, HD), BF16)

    def head(h):
        for i in reversed(range(toks // tb)):
            tok = pl.ds(i * tb, tb)
            cols = pl.ds(i * step, step)
            seen = (i + 1) * tb
            q = q_ref[tok, h].reshape(step, HD)
            go = go_ref[tok, h].reshape(step, HD)
            prod = go.astype(F32) * ao_ref[tok, h].reshape(step, HD).astype(F32)
            high = prod.astype(BF16)
            low = (prod - high.astype(F32)).astype(BF16)
            delta = (dot(ones, high, NT) + dot(ones, low, NT))[0:1]
            del_ref[h, :, cols] = delta
            k, v = rk_ref[h, :seen], rv_ref[h, :seen]
            s = dot(k, q, NT) * (SCALE * LOG2E) - lse_ref[h, :, cols]
            p = jnp.exp2(s)
            key = lax.broadcasted_iota(jnp.int32, (tb, step), 0)
            query = lax.broadcasted_iota(jnp.int32, (tb, step), 1) // QPK
            edge = jnp.where(key <= query, p[i * tb :], 0.0)
            p = jnp.concatenate([p[: i * tb], edge], 0) if i else edge
            ds = p * (dot(v, go, NT) - delta)
            pb, dsb = p.astype(BF16), ds.astype(BF16)
            ds_ref[h, :seen, cols] = dsb
            if seen < toks:
                ds_ref[h, seen:, cols] = jnp.zeros((toks - seen, step), BF16)
                dk_ref[h, :seen] += dot(dsb, q, NN)
                dv_ref[h, :seen] += dot(pb, go, NN)
            else:
                dk_ref[h] = dot(dsb, q, NN)
                dv_ref[h] = dot(pb, go, NN)

    loop(head)


def resp_grads(q, go, ao, lse, rk, rv):
    toks = q.shape[0]
    rows = toks * QPK
    return pl.pallas_call(
        functools.partial(resp_body, 1024),
        in_specs=[WHOLE] * 6,
        out_specs=[WHOLE] * 4,
        out_shape=[
            jax.ShapeDtypeStruct((HEADS, 1, rows), F32),
            jax.ShapeDtypeStruct((HEADS, toks, rows), BF16),
            jax.ShapeDtypeStruct((HEADS, toks, HD), F32),
            jax.ShapeDtypeStruct((HEADS, toks, HD), F32),
        ],
        compiler_params=pltpu.CompilerParams(vmem_limit_bytes=GRANT << 20),
        cost_estimate=cost(5 * 10**9, 1 << 20),
        name="resp",
    )(q, go, ao, lse, rk, rv)


def shard_keys(refs, h):
    k, v = [], []
    for r in refs:
        for at in range(0, r.shape[0], PAY):
            k.append(r[pl.ds(pl.multiple_of(at + h * SHARD, 16), SHARD)])
            v.append(r[pl.ds(pl.multiple_of(at + ROWS + h * SHARD, 16), SHARD)])
    return jnp.concatenate(k, 0), jnp.concatenate(v, 0)


def shard_rewards(refs):
    got = []
    for r in refs:
        for at in range(0, r.shape[0], PAY):
            tail = r[pl.ds(at + KV, 16)].astype(F32)
            got.append((tail[0:1] * 32.0 + tail[1:2], tail[2:3]))
    return got


def prompt_body(step, n, waits, notes, last, q_ref, go_ref, lse_ref, del_ref, stat_in, *refs):
    aux = refs[0] if last else None
    refs = refs[1:] if last else refs
    kv, refs = refs[:n], refs[n + waits :]
    ds_ref, outs, stat_ref = refs[0], refs[1:-1], refs[-1]
    toks = q_ref.shape[0]
    tb = step // QPK
    got = shard_rewards(kv)
    total, square = stat_in[0:1], stat_in[1:2]
    for r, _ in got:
        total, square = total + r, square + r * r
    stat_ref[...] = stat_in[...]
    stat_ref[0:1], stat_ref[1:2] = total, square
    for at, which in enumerate(notes):
        stat_ref[2 * at + 2 : 2 * at + 3], stat_ref[2 * at + 3 : 2 * at + 4] = got[which]
    factor = None
    if last:
        members = float(RING * PAIR)
        whole, pairs = total.astype(jnp.int32), square.astype(jnp.int32)
        spare = (RING * PAIR * pairs - whole * whole).astype(F32)
        spread = jnp.sqrt(jnp.maximum(spare, 0.0)) * (1.0 / (members * 256.0))
        weight = aux[2:3] / jnp.maximum(spread, 1.0)
        coefs = []
        for r, length in ((aux[0:1], aux[1:2]), (stat_in[2:3], stat_in[3:4]), (stat_in[4:5], stat_in[5:6])):
            coefs.append((r * members - total) * (1.0 / (members * 256.0)) * weight / length)
        for at, c in enumerate(coefs):
            stat_ref[at : at + 1] = c
        factor = coefs[0]

    def head(h):
        k, v = shard_keys(kv, h)
        dk = dv = None
        for i in range(toks // tb):
            tok = pl.ds(i * tb, tb)
            cols = pl.ds(i * step, step)
            q = q_ref[tok, h].reshape(step, HD)
            go = go_ref[tok, h].reshape(step, HD)
            p = jnp.exp2(dot(k, q, NT) * (SCALE * LOG2E) - lse_ref[h, :, cols])
            ds = p * (dot(v, go, NT) - del_ref[h, :, cols])
            pb, dsb = p.astype(BF16), ds.astype(BF16)
            ds_ref[h, :, cols] = dsb
            a, b = dot(dsb, q, NN), dot(pb, go, NN)
            dk, dv = (a, b) if dk is None else (dk + a, dv + b)
        dk = dk * SCALE
        if last:
            dk, dv = dk * factor, dv * factor
        at = 0
        for out in outs:
            for y in range(out.shape[0]):
                out[y, 0, h] = dk[at : at + SHARD].astype(BF16)
                out[y, 1, h] = dv[at : at + SHARD].astype(BF16)
                at += SHARD

    loop(head)


def prompt_grads(name, q, go, lse, delta, stat, aux, shards, notes, apart, last, *waits):
    rows = q.shape[0] * QPK
    keys = len(shards) * PAIR * SHARD
    extra = [aux] if last else []
    ins = [q, go, lse, delta, stat, *extra, *shards]
    sizes = [PAIR] * len(shards)
    sizes = sizes[:-1] + [1] * PAIR if apart else sizes
    sums = [jax.ShapeDtypeStruct((n, 2, HEADS, SHARD, HD), BF16) for n in sizes]
    got = pl.pallas_call(
        functools.partial(prompt_body, 1024, len(shards), len(waits), notes, last),
        in_specs=[WHOLE] * len(ins) + [pl.BlockSpec(memory_space=pl.ANY)] * len(waits),
        out_specs=[WHOLE] * (len(sums) + 2),
        out_shape=[
            jax.ShapeDtypeStruct((HEADS, keys, rows), BF16),
            *sums,
            jax.ShapeDtypeStruct((8, HD), F32),
        ],
        compiler_params=pltpu.CompilerParams(vmem_limit_bytes=GRANT << 20),
        cost_estimate=cost((keys // 192) * 5 * 10**9 + 10**8, 1 << 20),
        name=name,
    )(*ins, *waits)
    return got[0], [x.reshape(x.shape[0] * KV, HD) for x in got[1:-1]], got[-1]


def query_body(head, n_ds, counts, ins, coef_ref, *refs):
    ds, shards, rk_ref = refs[:n_ds], refs[n_ds : n_ds + sum(counts)], refs[n_ds + sum(counts)]
    out, coef_out, rows_ref, sems = refs[ins - 1 :]
    step = 512
    tb = step // QPK
    keys, at = [], 0
    for c in counts:
        keys.append(shard_keys(shards[at : at + c], head)[0])
        at += c
    keys.append(rk_ref[head])
    coef_out[...] = coef_ref[...]
    factor = coef_ref[0:1] * SCALE
    sends = []
    for i in range(ds[0].shape[2] // step):
        acc = None
        for d, k in zip(ds, keys):
            a = dot(k, d[head, :, pl.ds(i * step, step)], TN)
            acc = a if acc is None else acc + a
        rows_ref[i * tb : (i + 1) * tb] = (acc.T * factor).astype(BF16).reshape(tb, QPK, HD)
        tok = pl.ds(i * tb, tb)
        sends.append(pltpu.make_async_copy(rows_ref.at[tok], out.at[tok, head], sems.at[i]))
        sends[-1].start()
    for send in sends:
        send.wait()


def query_grads(head, coef, ds, groups, rk, so_far, *waits):
    toks = ds[0].shape[2] // QPK
    counts = [len(g) for g in groups]
    shards = [s for g in groups for s in g]
    there = pl.BlockSpec(memory_space=pl.ANY)
    ins = [coef, *ds, *shards, rk]
    specs = [WHOLE] * len(ins) + [there] * len(waits)
    ins += waits
    alias = {}
    if so_far is not None:
        alias = {len(ins): 0}
        ins.append(so_far)
        specs.append(there)
    return pl.pallas_call(
        functools.partial(query_body, head, len(ds), counts, len(ins)),
        in_specs=specs,
        out_specs=[there, WHOLE],
        out_shape=[
            jax.ShapeDtypeStruct((toks, HEADS, QPK, HD), BF16),
            jax.ShapeDtypeStruct((8, HD), F32),
        ],
        input_output_aliases=alias,
        scratch_shapes=[pltpu.VMEM((toks, QPK, HD), BF16), pltpu.SemaphoreType.DMA((4,))],
        compiler_params=pltpu.CompilerParams(vmem_limit_bytes=GRANT << 20),
        cost_estimate=cost(4 * 10**9, 1 << 20),
        name="dq",
    )(*ins)


def out_body(coef_ref, dk_ref, dv_ref, drk_ref, drv_ref, coef_out):
    coef_out[...] = coef_ref[...]
    factor = coef_ref[0:1]
    for src, dst, c in ((dk_ref, drk_ref, factor * SCALE), (dv_ref, drv_ref, factor)):
        dst[...] = jnp.transpose(src[...] * c, (1, 0, 2)).astype(BF16)


def resp_out(coef, dk, dv):
    out = jax.ShapeDtypeStruct((dk.shape[1], HEADS, HD), BF16)
    return pl.pallas_call(
        out_body,
        in_specs=[WHOLE] * 3,
        out_specs=[WHOLE] * 3,
        out_shape=[out, out, jax.ShapeDtypeStruct((8, HD), F32)],
        compiler_params=pltpu.CompilerParams(vmem_limit_bytes=GRANT << 20),
        cost_estimate=cost(4 * 10**9, 1 << 20),
        name="out",
    )(coef, dk, dv)


def hop(x, dz, dy=0):
    pairs = [
        (z * PAIR + y, ((z + dz) % RING) * PAIR + (y + dy) % PAIR)
        for z in range(RING)
        for y in range(PAIR)
    ]
    return lax.ppermute(x, "group", pairs)


def swap_core(x):
    return lax.ppermute(x, "tensor", [(0, 1), (1, 0)])


def in_order(core, mine, other, axis):
    return jnp.where(
        core == 0,
        jnp.concatenate([mine, other], axis),
        jnp.concatenate([other, mine], axis),
    )


def on_device(
    queries,
    resp_keys,
    resp_values,
    prompt_keys,
    prompt_values,
    attn_out,
    grad_out,
    log_sums,
    prompt_lengths,
    resp_lengths,
    rewards,
    task_ids,
    task_weights,
):
    core = lax.axis_index("tensor")
    member = lax.axis_index("group")
    toks = queries.shape[2]
    part = prompt_keys.shape[1]
    length = resp_lengths[0, 0]
    reward = rewards[0, 0]

    mine, theirs = split_heads(prompt_lengths, prompt_keys, prompt_values)
    own = join_tokens(rewards, resp_lengths, mine, swap_core(theirs))

    q, go, ao = queries[0, 0], grad_out[0, 0], attn_out[0, 0]
    rk, rv, lse, aux = resp_rows(
        rewards,
        resp_lengths,
        task_ids,
        task_weights,
        own,
        resp_keys[0, 0],
        resp_values[0, 0],
        log_sums[0, 0],
    )
    stat = jnp.zeros((8, HD), F32)

    delta, ds_r, dk_r, dv_r = resp_grads(q, go, ao, lse, rk, rv)
    pair = join_pair(lse, own, hop(own, 0, 1))
    back1, fore1 = hop(pair, 1), hop(pair, -1)
    far = hop(pair, 4)
    back2, fore2 = hop(back1, 1), hop(fore1, -1)
    back3, fore3 = hop(back2, 1), hop(fore2, -1)

    common = (q, go, lse, delta)
    ds_1, (here, down_1, up_1), stat = prompt_grads(
        "near", *common, stat, None, [pair, back1, fore1], (PAIR, 2 * PAIR), False, False, far
    )
    ds_2, (down_2, up_2, down_4, up_4), stat = prompt_grads(
        "second", *common, stat, None, [back2, fore2, far], (), True, False
    )
    down_4, up_4 = hop(down_4, -1), hop(up_4, 1)
    ds_3, (down_3, up_3), coef = prompt_grads(
        "third", *common, stat, aux, [back3, fore3], (), False, True
    )

    groups = [[pair, back1, fore1], [back2, fore2, far], [back3, fore3]]
    ds_all = [ds_1, ds_2, ds_3, ds_r]

    def dq(head, so_far, *waits):
        return query_grads(head, coef, ds_all, groups, rk, so_far, *waits)

    def add(a, c, b):
        return (a.astype(F32) + c[0:1] * b.astype(F32)).astype(BF16)

    down = jnp.concatenate([add(down_3[:KV], coef[2:3], down_4), down_3[KV:]], 0)
    up = jnp.concatenate([up_3[:KV], add(up_3[KV:], coef[1:2], up_4)], 0)
    down, up = hop(down, -1), hop(up, 1)
    grad_q, _ = dq(0, None)
    grad_q, again = dq(1, grad_q)
    down, up = add(down, again, down_2), add(up, again, up_2)
    grad_q, again = dq(2, grad_q, down, up)
    drk, drv, again = resp_out(again, dk_r, dv_r)
    down, up = hop(down, -1), hop(up, 1)
    down, up = add(down, again, down_1), add(up, again, up_1)
    grad_q, again = dq(3, grad_q, down, up)
    down, up = hop(down, -1), hop(up, 1)
    home = again[0:1] * here.astype(F32)
    home = home + down.astype(F32) + up.astype(F32)
    beside = hop(home[KV:].astype(BF16), 0, 1)
    home = (home[:KV] + beside.astype(F32)).reshape(2, HEADS, 2, part, HD)
    keep = lax.dynamic_index_in_dim(home, core, 2, keepdims=False)
    give = lax.dynamic_index_in_dim(home, 1 - core, 2, keepdims=False)
    take = swap_core(give)
    done = in_order(core, keep, take, 1).transpose(0, 2, 1, 3).astype(BF16)
    slot = (member * 2 + core) * part + jnp.arange(part)
    done = jnp.where((slot < prompt_lengths[0])[None, :, None, None], done, 0)
    return (
        grad_q.reshape(1, 1, toks, HEADS, QPK, HD),
        drk[None, None],
        drv[None, None],
        done[0][None],
        done[1][None],
    )


def solution(mesh):
    wide = P("prompt", "group", None, "tensor", None, None)
    resp = P("prompt", "group", None, "tensor", None)
    prompt = P("prompt", ("group", "tensor"), None, None)
    return jax.shard_map(
        on_device,
        mesh=mesh,
        in_specs=(
            wide,
            resp,
            resp,
            prompt,
            prompt,
            wide,
            wide,
            P("prompt", "group", "tensor", None, None),
            P("prompt"),
            P("prompt", "group"),
            P("prompt", "group"),
            P("prompt"),
            P(),
        ),
        out_specs=(wide, resp, resp, prompt, prompt),
        check_vma=False,
    )
```

```python
import functools
import math

import jax
import jax.numpy as jnp
from jax import lax
from jax.experimental import pallas as pl
from jax.experimental.pallas import tpu as pltpu
from jax.sharding import PartitionSpec as P

HEADS = 4
QPK = 8
HD = 128
SHARD = 48
ROWS = HEADS * SHARD
KV = 2 * ROWS
PAY = KV + 16
RING = 8
PAIR = 2
SCALE = HD ** (-0.5)
LOG2E = math.log2(math.e)
DEAD = 1e30
WHOLE = pl.BlockSpec(memory_space=pltpu.VMEM)
GRANT = 20
SMALL = 4
NT = (((1,), (1,)), ((), ()))
NN = (((1,), (0,)), ((), ()))
TN = (((0,), (0,)), ((), ()))
F32, BF16 = jnp.float32, jnp.bfloat16


def dot(a, b, dims):
    return lax.dot_general(a, b, dims, preferred_element_type=F32)


def cost(flops, traffic):
    return pl.CostEstimate(flops=flops, bytes_accessed=traffic, transcendentals=0)


def split_body(live_ref, pk_ref, pv_ref, mine_ref, theirs_ref):
    core, member = lax.axis_index("tensor"), lax.axis_index("group")
    part = pk_ref.shape[1]
    slot = (member * 2 + core) * part + lax.broadcasted_iota(jnp.int32, pk_ref.shape[1:], 0)
    keys = jnp.where(slot < live_ref[0], pk_ref[0].astype(F32), 0.0)
    for at, x in enumerate((keys, pv_ref[0].astype(F32))):
        x = jnp.transpose(x, (1, 0, 2))
        low, high = x[:HEADS], x[HEADS:]
        mine_ref[at] = jnp.where(core == 0, low, high)
        theirs_ref[at] = jnp.where(core == 0, high, low)


def split_heads(live, pk, pv):
    part = pk.shape[1]
    whole = pl.BlockSpec(memory_space=pltpu.VMEM)
    half = jax.ShapeDtypeStruct((2, HEADS, part, HD), F32)
    return pl.pallas_call(
        split_body,
        in_specs=[pl.BlockSpec(memory_space=pltpu.SMEM), whole, whole],
        out_specs=[whole, whole],
        out_shape=[half, half],
        compiler_params=pltpu.CompilerParams(vmem_limit_bytes=SMALL << 20),
        name="split",
    )(live, pk, pv)


def join_body(reward_ref, length_ref, mine_ref, got_ref, out_ref):
    core = lax.axis_index("tensor")
    for at in range(2):
        for h in range(HEADS):
            a, b = mine_ref[at, h], got_ref[at, h]
            pair = [jnp.where(core == 0, a, b), jnp.where(core == 0, b, a)]
            first = (at * HEADS + h) * SHARD
            out_ref[first : first + SHARD] = jnp.concatenate(pair, 0).astype(BF16)
    reward, length = reward_ref[0, 0], length_ref[0, 0]
    line = lax.broadcasted_iota(jnp.int32, (16, HD), 0)
    note = jnp.where(line == 0, reward >> 5, jnp.where(line == 1, reward & 31, length))
    out_ref[KV:] = note.astype(F32).astype(BF16)


def join_tokens(reward, length, mine, got):
    whole = pl.BlockSpec(memory_space=pltpu.VMEM)
    number = pl.BlockSpec(memory_space=pltpu.SMEM)
    return pl.pallas_call(
        join_body,
        in_specs=[number] * 2 + [whole] * 2,
        out_specs=whole,
        out_shape=jax.ShapeDtypeStruct((PAY, HD), BF16),
        compiler_params=pltpu.CompilerParams(vmem_limit_bytes=SMALL << 20),
        name="join",
    )(reward, length, mine, got)


def pair_body(wait_ref, own_ref, beside_ref, out_ref):
    out_ref[:PAY] = own_ref[...]
    out_ref[PAY:] = beside_ref[...]


def join_pair(wait, own, beside):
    return pl.pallas_call(
        pair_body,
        in_specs=[pl.BlockSpec(memory_space=pl.ANY), WHOLE, WHOLE],
        out_specs=WHOLE,
        out_shape=jax.ShapeDtypeStruct((PAIR * PAY, HD), BF16),
        compiler_params=pltpu.CompilerParams(vmem_limit_bytes=SMALL << 20),
        name="pair",
    )(wait, own, beside)


def rows_body(reward_ref, length_ref, task_ref, weights_ref, wait_ref, rk_ref, rv_ref, lse_ref, *refs):
    rkt_ref, rvt_ref, row_ref, aux_ref = refs
    toks = rk_ref.shape[0]
    rows = toks * QPK
    weight = jnp.float32(0.0)
    for kind in range(weights_ref.shape[0]):
        weight = jnp.where(task_ref[0] == kind, weights_ref[kind], weight)
    line = lax.broadcasted_iota(jnp.int32, (8, HD), 0)
    note = jnp.where(line == 0, reward_ref[0, 0], length_ref[0, 0]).astype(F32)
    aux_ref[...] = jnp.where(line < 2, note, weight)
    for src, dst in ((rk_ref, rkt_ref), (rv_ref, rvt_ref)):
        dst[...] = jnp.transpose(src[...].astype(F32), (1, 0, 2)).astype(BF16)
    spread = lax.broadcasted_iota(jnp.int32, (toks, rows), 1) // QPK
    spread = (spread == lax.broadcasted_iota(jnp.int32, (toks, rows), 0)).astype(BF16)
    parts = []
    for h in range(HEADS):
        x = lse_ref[h] * LOG2E
        for _ in range(3):
            parts.append(x.astype(BF16))
            x = x - parts[-1].astype(F32)
    wide = dot(jnp.concatenate(parts, 0), spread, NN)
    line = lax.broadcasted_iota(jnp.int32, (QPK, rows), 0)
    lane = lax.broadcasted_iota(jnp.int32, (QPK, rows), 1)
    for h in range(HEADS):
        at = h * 3 * QPK
        x = wide[at : at + QPK] + (wide[at + QPK : at + 2 * QPK] + wide[at + 2 * QPK : at + 3 * QPK])
        x = jnp.sum(jnp.where(lane % QPK == line, x, 0.0), axis=0, keepdims=True)
        row_ref[h] = jnp.where(lane[0:1] // QPK < length_ref[0, 0], x, DEAD)


def resp_rows(reward, length, task, weights, wait, rk, rv, lse):
    toks = rk.shape[0]
    by_head = jax.ShapeDtypeStruct((HEADS, toks, HD), BF16)
    return pl.pallas_call(
        rows_body,
        in_specs=[pl.BlockSpec(memory_space=pltpu.SMEM)] * 4
        + [pl.BlockSpec(memory_space=pl.ANY)]
        + [WHOLE] * 3,
        out_specs=[WHOLE] * 4,
        out_shape=[
            by_head,
            by_head,
            jax.ShapeDtypeStruct((HEADS, 1, toks * QPK), F32),
            jax.ShapeDtypeStruct((8, HD), F32),
        ],
        compiler_params=pltpu.CompilerParams(vmem_limit_bytes=GRANT << 20),
        cost_estimate=cost(5 * 10**9, 1 << 20),
        name="rows",
    )(reward, length, task, weights, wait, rk, rv, lse)


def loop(body):
    lax.fori_loop(0, HEADS, lambda h, c: (body(h), c)[1], 0)


def resp_body(step, wait_ref, q_ref, go_ref, ao_ref, lse_ref, rk_ref, rv_ref, del_ref, ds_ref, dk_ref, dv_ref):
    toks = q_ref.shape[0]
    tb = step // QPK
    ones = jnp.ones((8, HD), BF16)

    def head(h):
        for i in reversed(range(toks // tb)):
            tok = pl.ds(i * tb, tb)
            cols = pl.ds(i * step, step)
            seen = (i + 1) * tb
            q = q_ref[tok, h].reshape(step, HD)
            go = go_ref[tok, h].reshape(step, HD)
            prod = go.astype(F32) * ao_ref[tok, h].reshape(step, HD).astype(F32)
            high = prod.astype(BF16)
            low = (prod - high.astype(F32)).astype(BF16)
            delta = (dot(ones, high, NT) + dot(ones, low, NT))[0:1]
            del_ref[h, :, cols] = delta
            k, v = rk_ref[h, :seen], rv_ref[h, :seen]
            s = dot(k, q, NT) * (SCALE * LOG2E) - lse_ref[h, :, cols]
            p = jnp.exp2(s)
            key = lax.broadcasted_iota(jnp.int32, (tb, step), 0)
            query = lax.broadcasted_iota(jnp.int32, (tb, step), 1) // QPK
            edge = jnp.where(key <= query, p[i * tb :], 0.0)
            p = jnp.concatenate([p[: i * tb], edge], 0) if i else edge
            ds = p * (dot(v, go, NT) - delta)
            pb, dsb = p.astype(BF16), ds.astype(BF16)
            ds_ref[h, :seen, cols] = dsb
            if seen < toks:
                ds_ref[h, seen:, cols] = jnp.zeros((toks - seen, step), BF16)
                dk_ref[h, :seen] += dot(dsb, q, NN)
                dv_ref[h, :seen] += dot(pb, go, NN)
            else:
                dk_ref[h] = dot(dsb, q, NN)
                dv_ref[h] = dot(pb, go, NN)

    loop(head)


def resp_grads(wait, q, go, ao, lse, rk, rv):
    toks = q.shape[0]
    rows = toks * QPK
    return pl.pallas_call(
        functools.partial(resp_body, 1024),
        in_specs=[pl.BlockSpec(memory_space=pl.ANY)] + [WHOLE] * 6,
        out_specs=[WHOLE] * 4,
        out_shape=[
            jax.ShapeDtypeStruct((HEADS, 1, rows), F32),
            jax.ShapeDtypeStruct((HEADS, toks, rows), BF16),
            jax.ShapeDtypeStruct((HEADS, toks, HD), F32),
            jax.ShapeDtypeStruct((HEADS, toks, HD), F32),
        ],
        compiler_params=pltpu.CompilerParams(vmem_limit_bytes=GRANT << 20),
        cost_estimate=cost(5 * 10**9, 1 << 20),
        name="resp",
    )(wait, q, go, ao, lse, rk, rv)


def shard_keys(refs, h):
    k, v = [], []
    for r in refs:
        for at in range(0, r.shape[0], PAY):
            k.append(r[pl.ds(pl.multiple_of(at + h * SHARD, 16), SHARD)])
            v.append(r[pl.ds(pl.multiple_of(at + ROWS + h * SHARD, 16), SHARD)])
    return jnp.concatenate(k, 0), jnp.concatenate(v, 0)


def shard_rewards(refs):
    got = []
    for r in refs:
        for at in range(0, r.shape[0], PAY):
            tail = r[pl.ds(at + KV, 16)].astype(F32)
            got.append((tail[0:1] * 32.0 + tail[1:2], tail[2:3]))
    return got


def prompt_body(step, n, waits, notes, last, q_ref, go_ref, lse_ref, del_ref, stat_in, *refs):
    aux = refs[0] if last else None
    refs = refs[1:] if last else refs
    kv, refs = refs[:n], refs[n + waits :]
    ds_ref, outs, stat_ref = refs[0], refs[1:-1], refs[-1]
    toks = q_ref.shape[0]
    tb = step // QPK
    got = shard_rewards(kv)
    total, square = stat_in[0:1], stat_in[1:2]
    for r, _ in got:
        total, square = total + r, square + r * r
    stat_ref[...] = stat_in[...]
    stat_ref[0:1], stat_ref[1:2] = total, square
    for at, which in enumerate(notes):
        stat_ref[2 * at + 2 : 2 * at + 3], stat_ref[2 * at + 3 : 2 * at + 4] = got[which]
    factor = None
    if last:
        members = float(RING * PAIR)
        whole, pairs = total.astype(jnp.int32), square.astype(jnp.int32)
        spare = (RING * PAIR * pairs - whole * whole).astype(F32)
        spread = jnp.sqrt(jnp.maximum(spare, 0.0)) * (1.0 / (members * 256.0))
        weight = aux[2:3] / jnp.maximum(spread, 1.0)
        coefs = []
        for r, length in ((aux[0:1], aux[1:2]), (stat_in[2:3], stat_in[3:4]), (stat_in[4:5], stat_in[5:6])):
            coefs.append((r * members - total) * (1.0 / (members * 256.0)) * weight / length)
        for at, c in enumerate(coefs):
            stat_ref[at : at + 1] = c
        factor = coefs[0]

    def head(h):
        k, v = shard_keys(kv, h)
        dk = dv = None
        for i in range(toks // tb):
            tok = pl.ds(i * tb, tb)
            cols = pl.ds(i * step, step)
            q = q_ref[tok, h].reshape(step, HD)
            go = go_ref[tok, h].reshape(step, HD)
            p = jnp.exp2(dot(k, q, NT) * (SCALE * LOG2E) - lse_ref[h, :, cols])
            ds = p * (dot(v, go, NT) - del_ref[h, :, cols])
            pb, dsb = p.astype(BF16), ds.astype(BF16)
            ds_ref[h, :, cols] = dsb
            a, b = dot(dsb, q, NN), dot(pb, go, NN)
            dk, dv = (a, b) if dk is None else (dk + a, dv + b)
        dk = dk * SCALE
        if last:
            dk, dv = dk * factor, dv * factor
        at = 0
        for out in outs:
            for y in range(out.shape[0]):
                out[y, 0, h] = dk[at : at + SHARD].astype(BF16)
                out[y, 1, h] = dv[at : at + SHARD].astype(BF16)
                at += SHARD

    loop(head)


def prompt_grads(name, q, go, lse, delta, stat, aux, shards, notes, last, *waits):
    rows = q.shape[0] * QPK
    keys = sum(x.shape[0] // PAY for x in shards) * SHARD
    extra = [aux] if last else []
    ins = [q, go, lse, delta, stat, *extra, *shards]
    sizes = [x.shape[0] // PAY for x in shards]
    sums = [jax.ShapeDtypeStruct((n, 2, HEADS, SHARD, HD), BF16) for n in sizes]
    got = pl.pallas_call(
        functools.partial(prompt_body, 1024, len(shards), len(waits), notes, last),
        in_specs=[WHOLE] * len(ins) + [pl.BlockSpec(memory_space=pl.ANY)] * len(waits),
        out_specs=[WHOLE] * (len(sums) + 2),
        out_shape=[
            jax.ShapeDtypeStruct((HEADS, keys, rows), BF16),
            *sums,
            jax.ShapeDtypeStruct((8, HD), F32),
        ],
        compiler_params=pltpu.CompilerParams(vmem_limit_bytes=GRANT << 20),
        cost_estimate=cost((keys // 192) * 5 * 10**9 + 10**8, 1 << 20),
        name=name,
    )(*ins, *waits)
    return got[0], [x.reshape(x.shape[0] * KV, HD) for x in got[1:-1]], got[-1]


def query_body(head, n_ds, counts, ins, coef_ref, *refs):
    ds, shards, rk_ref = refs[:n_ds], refs[n_ds : n_ds + sum(counts)], refs[n_ds + sum(counts)]
    out, coef_out, rows_ref, sems = refs[ins - 1 :]
    step = 512
    tb = step // QPK
    keys, at = [], 0
    for c in counts:
        keys.append(shard_keys(shards[at : at + c], head)[0])
        at += c
    keys.append(rk_ref[head])
    coef_out[...] = coef_ref[...]
    factor = coef_ref[0:1] * SCALE
    sends = []
    for i in range(ds[0].shape[2] // step):
        acc = None
        for d, k in zip(ds, keys):
            a = dot(k, d[head, :, pl.ds(i * step, step)], TN)
            acc = a if acc is None else acc + a
        rows_ref[i * tb : (i + 1) * tb] = (acc.T * factor).astype(BF16).reshape(tb, QPK, HD)
        tok = pl.ds(i * tb, tb)
        sends.append(pltpu.make_async_copy(rows_ref.at[tok], out.at[tok, head], sems.at[i]))
        sends[-1].start()
    for send in sends:
        send.wait()


def query_grads(head, coef, ds, groups, rk, so_far, *waits):
    toks = ds[0].shape[2] // QPK
    counts = [len(g) for g in groups]
    shards = [s for g in groups for s in g]
    there = pl.BlockSpec(memory_space=pl.ANY)
    ins = [coef, *ds, *shards, rk]
    specs = [WHOLE] * len(ins) + [there] * len(waits)
    ins += waits
    alias = {}
    if so_far is not None:
        alias = {len(ins): 0}
        ins.append(so_far)
        specs.append(there)
    return pl.pallas_call(
        functools.partial(query_body, head, len(ds), counts, len(ins)),
        in_specs=specs,
        out_specs=[there, WHOLE],
        out_shape=[
            jax.ShapeDtypeStruct((toks, HEADS, QPK, HD), BF16),
            jax.ShapeDtypeStruct((8, HD), F32),
        ],
        input_output_aliases=alias,
        scratch_shapes=[pltpu.VMEM((toks, QPK, HD), BF16), pltpu.SemaphoreType.DMA((4,))],
        compiler_params=pltpu.CompilerParams(vmem_limit_bytes=GRANT << 20),
        cost_estimate=cost(4 * 10**9, 1 << 20),
        name="dq",
    )(*ins)


def out_body(coef_ref, dk_ref, dv_ref, drk_ref, drv_ref, coef_out):
    coef_out[...] = coef_ref[...]
    factor = coef_ref[0:1]
    for src, dst, c in ((dk_ref, drk_ref, factor * SCALE), (dv_ref, drv_ref, factor)):
        dst[...] = jnp.transpose(src[...] * c, (1, 0, 2)).astype(BF16)


def resp_out(coef, dk, dv):
    out = jax.ShapeDtypeStruct((dk.shape[1], HEADS, HD), BF16)
    return pl.pallas_call(
        out_body,
        in_specs=[WHOLE] * 3,
        out_specs=[WHOLE] * 3,
        out_shape=[out, out, jax.ShapeDtypeStruct((8, HD), F32)],
        compiler_params=pltpu.CompilerParams(vmem_limit_bytes=GRANT << 20),
        cost_estimate=cost(4 * 10**9, 1 << 20),
        name="out",
    )(coef, dk, dv)


def hop(x, dz, dy=0):
    pairs = [
        (z * PAIR + y, ((z + dz) % RING) * PAIR + (y + dy) % PAIR)
        for z in range(RING)
        for y in range(PAIR)
    ]
    return lax.ppermute(x, "group", pairs)


def swap_core(x):
    return lax.ppermute(x, "tensor", [(0, 1), (1, 0)])


def in_order(core, mine, other, axis):
    return jnp.where(
        core == 0,
        jnp.concatenate([mine, other], axis),
        jnp.concatenate([other, mine], axis),
    )


def on_device(
    queries,
    resp_keys,
    resp_values,
    prompt_keys,
    prompt_values,
    attn_out,
    grad_out,
    log_sums,
    prompt_lengths,
    resp_lengths,
    rewards,
    task_ids,
    task_weights,
):
    core = lax.axis_index("tensor")
    member = lax.axis_index("group")
    toks = queries.shape[2]
    part = prompt_keys.shape[1]
    length = resp_lengths[0, 0]
    reward = rewards[0, 0]

    mine, theirs = split_heads(prompt_lengths, prompt_keys, prompt_values)
    own = join_tokens(rewards, resp_lengths, mine, swap_core(theirs))

    q, go, ao = queries[0, 0], grad_out[0, 0], attn_out[0, 0]
    rk, rv, lse, aux = resp_rows(
        rewards,
        resp_lengths,
        task_ids,
        task_weights,
        own,
        resp_keys[0, 0],
        resp_values[0, 0],
        log_sums[0, 0],
    )
    stat = jnp.zeros((8, HD), F32)

    far = hop(own, 4)
    delta, ds_r, dk_r, dv_r = resp_grads(far, q, go, ao, lse, rk, rv)
    pair = join_pair(lse, own, hop(own, 0, 1))
    back1, fore1 = hop(pair, 1), hop(pair, -1)
    far_x = hop(far, 0, 1)
    back2, fore2 = hop(back1, 1), hop(fore1, -1)
    back3, fore3 = hop(back2, 1), hop(fore2, -1)

    common = (q, go, lse, delta)
    ds_1, (here, down_1, up_1), stat = prompt_grads(
        "near", *common, stat, None, [pair, back1, fore1], (PAIR, 2 * PAIR), False
    )
    ds_2, (down_2, up_2, down_4, up_4), stat = prompt_grads(
        "second", *common, stat, None, [back2, fore2, far, far_x], (), False
    )
    down_4, up_4 = hop(down_4, -1), hop(up_4, 1)
    ds_3, (down_3, up_3), coef = prompt_grads(
        "third", *common, stat, aux, [back3, fore3], (), True
    )

    groups = [[pair, back1, fore1], [back2, fore2, far, far_x], [back3, fore3]]
    ds_all = [ds_1, ds_2, ds_3, ds_r]

    def dq(head, so_far, *waits):
        return query_grads(head, coef, ds_all, groups, rk, so_far, *waits)

    def add(a, c, b):
        return (a.astype(F32) + c[0:1] * b.astype(F32)).astype(BF16)

    down = jnp.concatenate([add(down_3[:KV], coef[2:3], down_4), down_3[KV:]], 0)
    up = jnp.concatenate([up_3[:KV], add(up_3[KV:], coef[1:2], up_4)], 0)
    down, up = hop(down, -1), hop(up, 1)
    grad_q, _ = dq(0, None)
    grad_q, again = dq(1, grad_q)
    down, up = add(down, again, down_2), add(up, again, up_2)
    grad_q, again = dq(2, grad_q, down, up)
    drk, drv, again = resp_out(again, dk_r, dv_r)
    down, up = hop(down, -1), hop(up, 1)
    down, up = add(down, again, down_1), add(up, again, up_1)
    grad_q, again = dq(3, grad_q, down, up)
    down, up = hop(down, -1), hop(up, 1)
    home = again[0:1] * here.astype(F32)
    home = home + down.astype(F32) + up.astype(F32)
    beside = hop(home[KV:].astype(BF16), 0, 1)
    home = (home[:KV] + beside.astype(F32)).reshape(2, HEADS, 2, part, HD)
    keep = lax.dynamic_index_in_dim(home, core, 2, keepdims=False)
    give = lax.dynamic_index_in_dim(home, 1 - core, 2, keepdims=False)
    take = swap_core(give)
    done = in_order(core, keep, take, 1).transpose(0, 2, 1, 3).astype(BF16)
    slot = (member * 2 + core) * part + jnp.arange(part)
    done = jnp.where((slot < prompt_lengths[0])[None, :, None, None], done, 0)
    return (
        grad_q.reshape(1, 1, toks, HEADS, QPK, HD),
        drk[None, None],
        drv[None, None],
        done[0][None],
        done[1][None],
    )


def solution(mesh):
    wide = P("prompt", "group", None, "tensor", None, None)
    resp = P("prompt", "group", None, "tensor", None)
    prompt = P("prompt", ("group", "tensor"), None, None)
    return jax.shard_map(
        on_device,
        mesh=mesh,
        in_specs=(
            wide,
            resp,
            resp,
            prompt,
            prompt,
            wide,
            wide,
            P("prompt", "group", "tensor", None, None),
            P("prompt"),
            P("prompt", "group"),
            P("prompt", "group"),
            P("prompt"),
            P(),
        ),
        out_specs=(wide, resp, resp, prompt, prompt),
        check_vma=False,
    )
```

```python
import functools
import math

import jax
import jax.numpy as jnp
from jax import lax
from jax.experimental import pallas as pl
from jax.experimental.pallas import tpu as pltpu
from jax.sharding import PartitionSpec as P

HEADS = 4
QPK = 8
HD = 128
SHARD = 48
ROWS = HEADS * SHARD
KV = 2 * ROWS
PAY = KV + 16
RING = 8
PAIR = 2
SCALE = HD ** (-0.5)
LOG2E = math.log2(math.e)
DEAD = 1e30
WHOLE = pl.BlockSpec(memory_space=pltpu.VMEM)
GRANT = 20
SMALL = 4
NT = (((1,), (1,)), ((), ()))
NN = (((1,), (0,)), ((), ()))
TN = (((0,), (0,)), ((), ()))
F32, BF16 = jnp.float32, jnp.bfloat16


def dot(a, b, dims):
    return lax.dot_general(a, b, dims, preferred_element_type=F32)


def cost(flops, traffic):
    return pl.CostEstimate(flops=flops, bytes_accessed=traffic, transcendentals=0)


def split_body(live_ref, pk_ref, pv_ref, mine_ref, theirs_ref):
    core, member = lax.axis_index("tensor"), lax.axis_index("group")
    part = pk_ref.shape[1]
    slot = (member * 2 + core) * part + lax.broadcasted_iota(jnp.int32, pk_ref.shape[1:], 0)
    keys = jnp.where(slot < live_ref[0], pk_ref[0].astype(F32), 0.0)
    for at, x in enumerate((keys, pv_ref[0].astype(F32))):
        x = jnp.transpose(x, (1, 0, 2))
        low, high = x[:HEADS], x[HEADS:]
        mine_ref[at] = jnp.where(core == 0, low, high)
        theirs_ref[at] = jnp.where(core == 0, high, low)


def split_heads(live, pk, pv):
    part = pk.shape[1]
    whole = pl.BlockSpec(memory_space=pltpu.VMEM)
    half = jax.ShapeDtypeStruct((2, HEADS, part, HD), F32)
    return pl.pallas_call(
        split_body,
        in_specs=[pl.BlockSpec(memory_space=pltpu.SMEM), whole, whole],
        out_specs=[whole, whole],
        out_shape=[half, half],
        compiler_params=pltpu.CompilerParams(vmem_limit_bytes=SMALL << 20),
        cost_estimate=cost(5 * 10**9, 1 << 20),
        name="split",
    )(live, pk, pv)


def join_body(reward_ref, length_ref, mine_ref, got_ref, out_ref):
    core = lax.axis_index("tensor")
    for at in range(2):
        for h in range(HEADS):
            a, b = mine_ref[at, h], got_ref[at, h]
            pair = [jnp.where(core == 0, a, b), jnp.where(core == 0, b, a)]
            first = (at * HEADS + h) * SHARD
            out_ref[first : first + SHARD] = jnp.concatenate(pair, 0).astype(BF16)
    reward, length = reward_ref[0, 0], length_ref[0, 0]
    line = lax.broadcasted_iota(jnp.int32, (16, HD), 0)
    note = jnp.where(line == 0, reward >> 5, jnp.where(line == 1, reward & 31, length))
    out_ref[KV:] = note.astype(F32).astype(BF16)


def join_tokens(reward, length, mine, got):
    whole = pl.BlockSpec(memory_space=pltpu.VMEM)
    number = pl.BlockSpec(memory_space=pltpu.SMEM)
    return pl.pallas_call(
        join_body,
        in_specs=[number] * 2 + [whole] * 2,
        out_specs=whole,
        out_shape=jax.ShapeDtypeStruct((PAY, HD), BF16),
        compiler_params=pltpu.CompilerParams(vmem_limit_bytes=SMALL << 20),
        cost_estimate=cost(5 * 10**9, 1 << 20),
        name="join",
    )(reward, length, mine, got)


def pair_body(wait_ref, own_ref, beside_ref, out_ref):
    out_ref[:PAY] = own_ref[...]
    out_ref[PAY:] = beside_ref[...]


def join_pair(wait, own, beside):
    return pl.pallas_call(
        pair_body,
        in_specs=[pl.BlockSpec(memory_space=pl.ANY), WHOLE, WHOLE],
        out_specs=WHOLE,
        out_shape=jax.ShapeDtypeStruct((PAIR * PAY, HD), BF16),
        compiler_params=pltpu.CompilerParams(vmem_limit_bytes=SMALL << 20),
        name="pair",
    )(wait, own, beside)


def rows_body(reward_ref, length_ref, task_ref, weights_ref, wait_ref, rk_ref, rv_ref, lse_ref, *refs):
    rkt_ref, rvt_ref, row_ref, aux_ref = refs
    toks = rk_ref.shape[0]
    rows = toks * QPK
    weight = jnp.float32(0.0)
    for kind in range(weights_ref.shape[0]):
        weight = jnp.where(task_ref[0] == kind, weights_ref[kind], weight)
    line = lax.broadcasted_iota(jnp.int32, (8, HD), 0)
    note = jnp.where(line == 0, reward_ref[0, 0], length_ref[0, 0]).astype(F32)
    aux_ref[...] = jnp.where(line < 2, note, weight)
    for src, dst in ((rk_ref, rkt_ref), (rv_ref, rvt_ref)):
        dst[...] = jnp.transpose(src[...].astype(F32), (1, 0, 2)).astype(BF16)
    spread = lax.broadcasted_iota(jnp.int32, (toks, rows), 1) // QPK
    spread = (spread == lax.broadcasted_iota(jnp.int32, (toks, rows), 0)).astype(BF16)
    parts = []
    for h in range(HEADS):
        x = lse_ref[h] * LOG2E
        for _ in range(3):
            parts.append(x.astype(BF16))
            x = x - parts[-1].astype(F32)
    wide = dot(jnp.concatenate(parts, 0), spread, NN)
    line = lax.broadcasted_iota(jnp.int32, (QPK, rows), 0)
    lane = lax.broadcasted_iota(jnp.int32, (QPK, rows), 1)
    for h in range(HEADS):
        at = h * 3 * QPK
        x = wide[at : at + QPK] + (wide[at + QPK : at + 2 * QPK] + wide[at + 2 * QPK : at + 3 * QPK])
        x = jnp.sum(jnp.where(lane % QPK == line, x, 0.0), axis=0, keepdims=True)
        row_ref[h] = jnp.where(lane[0:1] // QPK < length_ref[0, 0], x, DEAD)


def resp_rows(reward, length, task, weights, wait, rk, rv, lse):
    toks = rk.shape[0]
    by_head = jax.ShapeDtypeStruct((HEADS, toks, HD), BF16)
    return pl.pallas_call(
        rows_body,
        in_specs=[pl.BlockSpec(memory_space=pltpu.SMEM)] * 4
        + [pl.BlockSpec(memory_space=pl.ANY)]
        + [WHOLE] * 3,
        out_specs=[WHOLE] * 4,
        out_shape=[
            by_head,
            by_head,
            jax.ShapeDtypeStruct((HEADS, 1, toks * QPK), F32),
            jax.ShapeDtypeStruct((8, HD), F32),
        ],
        compiler_params=pltpu.CompilerParams(vmem_limit_bytes=GRANT << 20),
        cost_estimate=cost(5 * 10**9, 1 << 20),
        name="rows",
    )(reward, length, task, weights, wait, rk, rv, lse)


def loop(body):
    lax.fori_loop(0, HEADS, lambda h, c: (body(h), c)[1], 0)


def resp_body(step, wait_ref, q_ref, go_ref, ao_ref, lse_ref, rk_ref, rv_ref, del_ref, ds_ref, dk_ref, dv_ref):
    toks = q_ref.shape[0]
    tb = step // QPK
    ones = jnp.ones((8, HD), BF16)

    def head(h):
        for i in reversed(range(toks // tb)):
            tok = pl.ds(i * tb, tb)
            cols = pl.ds(i * step, step)
            seen = (i + 1) * tb
            q = q_ref[tok, h].reshape(step, HD)
            go = go_ref[tok, h].reshape(step, HD)
            prod = go.astype(F32) * ao_ref[tok, h].reshape(step, HD).astype(F32)
            high = prod.astype(BF16)
            low = (prod - high.astype(F32)).astype(BF16)
            delta = (dot(ones, high, NT) + dot(ones, low, NT))[0:1]
            del_ref[h, :, cols] = delta
            k, v = rk_ref[h, :seen], rv_ref[h, :seen]
            s = dot(k, q, NT) * (SCALE * LOG2E) - lse_ref[h, :, cols]
            p = jnp.exp2(s)
            key = lax.broadcasted_iota(jnp.int32, (tb, step), 0)
            query = lax.broadcasted_iota(jnp.int32, (tb, step), 1) // QPK
            edge = jnp.where(key <= query, p[i * tb :], 0.0)
            p = jnp.concatenate([p[: i * tb], edge], 0) if i else edge
            ds = p * (dot(v, go, NT) - delta)
            pb, dsb = p.astype(BF16), ds.astype(BF16)
            ds_ref[h, :seen, cols] = dsb
            if seen < toks:
                ds_ref[h, seen:, cols] = jnp.zeros((toks - seen, step), BF16)
                dk_ref[h, :seen] += dot(dsb, q, NN)
                dv_ref[h, :seen] += dot(pb, go, NN)
            else:
                dk_ref[h] = dot(dsb, q, NN)
                dv_ref[h] = dot(pb, go, NN)

    loop(head)


def resp_grads(wait, q, go, ao, lse, rk, rv):
    toks = q.shape[0]
    rows = toks * QPK
    return pl.pallas_call(
        functools.partial(resp_body, 1024),
        in_specs=[pl.BlockSpec(memory_space=pl.ANY)] + [WHOLE] * 6,
        out_specs=[WHOLE] * 4,
        out_shape=[
            jax.ShapeDtypeStruct((HEADS, 1, rows), F32),
            jax.ShapeDtypeStruct((HEADS, toks, rows), BF16),
            jax.ShapeDtypeStruct((HEADS, toks, HD), F32),
            jax.ShapeDtypeStruct((HEADS, toks, HD), F32),
        ],
        compiler_params=pltpu.CompilerParams(vmem_limit_bytes=GRANT << 20),
        cost_estimate=cost(5 * 10**9, 1 << 20),
        name="resp",
    )(wait, q, go, ao, lse, rk, rv)


def shard_keys(refs, h):
    k, v = [], []
    for r in refs:
        for at in range(0, r.shape[0], PAY):
            k.append(r[pl.ds(pl.multiple_of(at + h * SHARD, 16), SHARD)])
            v.append(r[pl.ds(pl.multiple_of(at + ROWS + h * SHARD, 16), SHARD)])
    return jnp.concatenate(k, 0), jnp.concatenate(v, 0)


def shard_rewards(refs):
    got = []
    for r in refs:
        for at in range(0, r.shape[0], PAY):
            tail = r[pl.ds(at + KV, 16)].astype(F32)
            got.append((tail[0:1] * 32.0 + tail[1:2], tail[2:3]))
    return got


def prompt_body(step, n, waits, notes, last, q_ref, go_ref, lse_ref, del_ref, stat_in, *refs):
    aux = refs[0] if last else None
    refs = refs[1:] if last else refs
    kv, refs = refs[:n], refs[n + waits :]
    ds_ref, outs, stat_ref = refs[0], refs[1:-1], refs[-1]
    toks = q_ref.shape[0]
    tb = step // QPK
    got = shard_rewards(kv)
    total, square = stat_in[0:1], stat_in[1:2]
    for r, _ in got:
        total, square = total + r, square + r * r
    stat_ref[...] = stat_in[...]
    stat_ref[0:1], stat_ref[1:2] = total, square
    for at, which in enumerate(notes):
        stat_ref[2 * at + 2 : 2 * at + 3], stat_ref[2 * at + 3 : 2 * at + 4] = got[which]
    factor = None
    if last:
        members = float(RING * PAIR)
        whole, pairs = total.astype(jnp.int32), square.astype(jnp.int32)
        spare = (RING * PAIR * pairs - whole * whole).astype(F32)
        spread = jnp.sqrt(jnp.maximum(spare, 0.0)) * (1.0 / (members * 256.0))
        weight = aux[2:3] / jnp.maximum(spread, 1.0)
        coefs = []
        for r, length in ((aux[0:1], aux[1:2]), (stat_in[2:3], stat_in[3:4]), (stat_in[4:5], stat_in[5:6])):
            coefs.append((r * members - total) * (1.0 / (members * 256.0)) * weight / length)
        for at, c in enumerate(coefs):
            stat_ref[at : at + 1] = c
        factor = coefs[0]

    def head(h):
        k, v = shard_keys(kv, h)
        dk = dv = None
        for i in range(toks // tb):
            tok = pl.ds(i * tb, tb)
            cols = pl.ds(i * step, step)
            q = q_ref[tok, h].reshape(step, HD)
            go = go_ref[tok, h].reshape(step, HD)
            p = jnp.exp2(dot(k, q, NT) * (SCALE * LOG2E) - lse_ref[h, :, cols])
            ds = p * (dot(v, go, NT) - del_ref[h, :, cols])
            pb, dsb = p.astype(BF16), ds.astype(BF16)
            ds_ref[h, :, cols] = dsb
            a, b = dot(dsb, q, NN), dot(pb, go, NN)
            dk, dv = (a, b) if dk is None else (dk + a, dv + b)
        dk = dk * SCALE
        if last:
            dk, dv = dk * factor, dv * factor
        at = 0
        for out in outs:
            for y in range(out.shape[0]):
                out[y, 0, h] = dk[at : at + SHARD].astype(BF16)
                out[y, 1, h] = dv[at : at + SHARD].astype(BF16)
                at += SHARD

    loop(head)


def prompt_grads(name, q, go, lse, delta, stat, aux, shards, notes, last, *waits):
    rows = q.shape[0] * QPK
    keys = sum(x.shape[0] // PAY for x in shards) * SHARD
    extra = [aux] if last else []
    ins = [q, go, lse, delta, stat, *extra, *shards]
    sizes = [x.shape[0] // PAY for x in shards]
    sums = [jax.ShapeDtypeStruct((n, 2, HEADS, SHARD, HD), BF16) for n in sizes]
    got = pl.pallas_call(
        functools.partial(prompt_body, 1024, len(shards), len(waits), notes, last),
        in_specs=[WHOLE] * len(ins) + [pl.BlockSpec(memory_space=pl.ANY)] * len(waits),
        out_specs=[WHOLE] * (len(sums) + 2),
        out_shape=[
            jax.ShapeDtypeStruct((HEADS, keys, rows), BF16),
            *sums,
            jax.ShapeDtypeStruct((8, HD), F32),
        ],
        compiler_params=pltpu.CompilerParams(vmem_limit_bytes=GRANT << 20),
        cost_estimate=cost((keys // 192) * 5 * 10**9 + 10**8, 1 << 20),
        name=name,
    )(*ins, *waits)
    return got[0], [x.reshape(x.shape[0] * KV, HD) for x in got[1:-1]], got[-1]


def query_body(head, n_ds, counts, ins, coef_ref, *refs):
    ds, shards, rk_ref = refs[:n_ds], refs[n_ds : n_ds + sum(counts)], refs[n_ds + sum(counts)]
    out, coef_out, rows_ref, sems = refs[ins - 1 :]
    step = 512
    tb = step // QPK
    keys, at = [], 0
    for c in counts:
        keys.append(shard_keys(shards[at : at + c], head)[0])
        at += c
    keys.append(rk_ref[head])
    coef_out[...] = coef_ref[...]
    factor = coef_ref[0:1] * SCALE
    sends = []
    for i in range(ds[0].shape[2] // step):
        acc = None
        for d, k in zip(ds, keys):
            a = dot(k, d[head, :, pl.ds(i * step, step)], TN)
            acc = a if acc is None else acc + a
        rows_ref[i * tb : (i + 1) * tb] = (acc.T * factor).astype(BF16).reshape(tb, QPK, HD)
        tok = pl.ds(i * tb, tb)
        sends.append(pltpu.make_async_copy(rows_ref.at[tok], out.at[tok, head], sems.at[i]))
        sends[-1].start()
    for send in sends:
        send.wait()


def query_grads(head, coef, ds, groups, rk, so_far, *waits):
    toks = ds[0].shape[2] // QPK
    counts = [len(g) for g in groups]
    shards = [s for g in groups for s in g]
    there = pl.BlockSpec(memory_space=pl.ANY)
    ins = [coef, *ds, *shards, rk]
    specs = [WHOLE] * len(ins) + [there] * len(waits)
    ins += waits
    alias = {}
    if so_far is not None:
        alias = {len(ins): 0}
        ins.append(so_far)
        specs.append(there)
    return pl.pallas_call(
        functools.partial(query_body, head, len(ds), counts, len(ins)),
        in_specs=specs,
        out_specs=[there, WHOLE],
        out_shape=[
            jax.ShapeDtypeStruct((toks, HEADS, QPK, HD), BF16),
            jax.ShapeDtypeStruct((8, HD), F32),
        ],
        input_output_aliases=alias,
        scratch_shapes=[pltpu.VMEM((toks, QPK, HD), BF16), pltpu.SemaphoreType.DMA((4,))],
        compiler_params=pltpu.CompilerParams(vmem_limit_bytes=GRANT << 20),
        cost_estimate=cost(4 * 10**9, 1 << 20),
        name="dq",
    )(*ins)


def out_body(coef_ref, dk_ref, dv_ref, drk_ref, drv_ref, coef_out):
    coef_out[...] = coef_ref[...]
    factor = coef_ref[0:1]
    for src, dst, c in ((dk_ref, drk_ref, factor * SCALE), (dv_ref, drv_ref, factor)):
        dst[...] = jnp.transpose(src[...] * c, (1, 0, 2)).astype(BF16)


def resp_out(coef, dk, dv):
    out = jax.ShapeDtypeStruct((dk.shape[1], HEADS, HD), BF16)
    return pl.pallas_call(
        out_body,
        in_specs=[WHOLE] * 3,
        out_specs=[WHOLE] * 3,
        out_shape=[out, out, jax.ShapeDtypeStruct((8, HD), F32)],
        compiler_params=pltpu.CompilerParams(vmem_limit_bytes=GRANT << 20),
        cost_estimate=cost(4 * 10**9, 1 << 20),
        name="out",
    )(coef, dk, dv)


def cut_body(coef_ref, here_ref, down_ref, up_ref, keep_ref, side_ref, other_ref, both_ref):
    core = lax.axis_index("tensor")
    part = SHARD // 2
    factor = coef_ref[0:1]
    for y, (stays, leaves) in enumerate(((keep_ref, other_ref), (side_ref, both_ref))):
        for at in range(2):
            for h in range(HEADS):
                first = y * KV + at * ROWS + h * SHARD
                rows = pl.ds(first, SHARD)
                x = factor * here_ref[rows].astype(F32)
                x = x + down_ref[rows].astype(F32) + up_ref[rows].astype(F32)
                a, b = x[:part], x[part:]
                stays[at, h] = jnp.where(core == 0, a, b)
                leaves[at, h] = jnp.where(core == 0, b, a)


def cut(coef, here, down, up):
    out = jax.ShapeDtypeStruct((2, HEADS, SHARD // 2, HD), F32)
    return pl.pallas_call(
        cut_body,
        in_specs=[WHOLE] * 4,
        out_specs=[WHOLE] * 4,
        out_shape=[out] * 4,
        compiler_params=pltpu.CompilerParams(vmem_limit_bytes=SMALL << 20),
        name="cut",
    )(coef, here, down, up)


def finish_body(live_ref, keep_ref, side_ref, other_ref, both_ref, pk_ref, pv_ref):
    core, member = lax.axis_index("tensor"), lax.axis_index("group")
    part = keep_ref.shape[2]
    shape = (part, 2 * HEADS, HD)
    slot = (member * 2 + core) * part + lax.broadcasted_iota(jnp.int32, shape, 0)
    for at, out in enumerate((pk_ref, pv_ref)):
        mine = keep_ref[at] + side_ref[at]
        theirs = other_ref[at] + both_ref[at]
        low = jnp.where(core == 0, mine, theirs)
        high = jnp.where(core == 0, theirs, mine)
        x = jnp.transpose(jnp.concatenate([low, high], 0), (1, 0, 2))
        out[0] = jnp.where(slot < live_ref[0], x, 0.0).astype(BF16)


def finish(live, keep, side, other, both):
    out = jax.ShapeDtypeStruct((1, keep.shape[2], 2 * HEADS, HD), BF16)
    return pl.pallas_call(
        finish_body,
        in_specs=[pl.BlockSpec(memory_space=pltpu.SMEM)] + [WHOLE] * 4,
        out_specs=[WHOLE] * 2,
        out_shape=[out] * 2,
        compiler_params=pltpu.CompilerParams(vmem_limit_bytes=SMALL << 20),
        name="finish",
    )(live, keep, side, other, both)


def hop(x, dz, dy=0):
    pairs = [
        (z * PAIR + y, ((z + dz) % RING) * PAIR + (y + dy) % PAIR)
        for z in range(RING)
        for y in range(PAIR)
    ]
    return lax.ppermute(x, "group", pairs)


def swap_core(x):
    return lax.ppermute(x, "tensor", [(0, 1), (1, 0)])


def swap_both(x):
    pairs = []
    for member in range(RING * PAIR):
        for core in range(2):
            pairs.append((member * 2 + core, (member ^ 1) * 2 + 1 - core))
    return lax.ppermute(x, ("group", "tensor"), pairs)


def on_device(
    queries,
    resp_keys,
    resp_values,
    prompt_keys,
    prompt_values,
    attn_out,
    grad_out,
    log_sums,
    prompt_lengths,
    resp_lengths,
    rewards,
    task_ids,
    task_weights,
):

    mine, theirs = split_heads(prompt_lengths, prompt_keys, prompt_values)
    own = join_tokens(rewards, resp_lengths, mine, swap_core(theirs))

    q, go, ao = queries[0, 0], grad_out[0, 0], attn_out[0, 0]
    rk, rv, lse, aux = resp_rows(
        rewards,
        resp_lengths,
        task_ids,
        task_weights,
        own,
        resp_keys[0, 0],
        resp_values[0, 0],
        log_sums[0, 0],
    )
    stat = jnp.zeros((8, HD), F32)

    far = hop(own, 4)
    delta, ds_r, dk_r, dv_r = resp_grads(far, q, go, ao, lse, rk, rv)
    pair = join_pair(lse, own, hop(own, 0, 1))
    back1, fore1 = hop(pair, 1), hop(pair, -1)
    far_x = hop(far, 0, 1)
    back2, fore2 = hop(back1, 1), hop(fore1, -1)
    back3, fore3 = hop(back2, 1), hop(fore2, -1)

    common = (q, go, lse, delta)
    ds_1, (here, down_1, up_1), stat = prompt_grads(
        "near", *common, stat, None, [pair, back1, fore1], (PAIR, 2 * PAIR), False
    )
    ds_2, (down_2, up_2, down_4, up_4), stat = prompt_grads(
        "second", *common, stat, None, [back2, fore2, far, far_x], (), False
    )
    down_4, up_4 = hop(down_4, -1), hop(up_4, 1)
    ds_3, (down_3, up_3), coef = prompt_grads(
        "third", *common, stat, aux, [back3, fore3], (), True
    )

    groups = [[pair, back1, fore1], [back2, fore2, far, far_x], [back3, fore3]]
    ds_all = [ds_1, ds_2, ds_3, ds_r]

    def dq(head, so_far, *waits):
        return query_grads(head, coef, ds_all, groups, rk, so_far, *waits)

    def add(a, c, b):
        return (a.astype(F32) + c[0:1] * b.astype(F32)).astype(BF16)

    down = jnp.concatenate([add(down_3[:KV], coef[2:3], down_4), down_3[KV:]], 0)
    up = jnp.concatenate([up_3[:KV], add(up_3[KV:], coef[1:2], up_4)], 0)
    down, up = hop(down, -1), hop(up, 1)
    grad_q, _ = dq(0, None)
    grad_q, again = dq(1, grad_q)
    down, up = add(down, again, down_2), add(up, again, up_2)
    grad_q, again = dq(2, grad_q, down, up)
    drk, drv, again = resp_out(again, dk_r, dv_r)
    down, up = hop(down, -1), hop(up, 1)
    down, up = add(down, again, down_1), add(up, again, up_1)
    grad_q, again = dq(3, grad_q, down, up)
    down, up = hop(down, -1), hop(up, 1)
    keep, side, other, both = cut(again, here, down, up)
    side, both = hop(side, 0, 1), swap_both(both)
    grad_pk, grad_pv = finish(prompt_lengths, keep, side, swap_core(other), both)
    return (
        grad_q[None, None],
        drk[None, None],
        drv[None, None],
        grad_pk,
        grad_pv,
    )


def solution(mesh):
    wide = P("prompt", "group", None, "tensor", None, None)
    resp = P("prompt", "group", None, "tensor", None)
    prompt = P("prompt", ("group", "tensor"), None, None)
    return jax.shard_map(
        on_device,
        mesh=mesh,
        in_specs=(
            wide,
            resp,
            resp,
            prompt,
            prompt,
            wide,
            wide,
            P("prompt", "group", "tensor", None, None),
            P("prompt"),
            P("prompt", "group"),
            P("prompt", "group"),
            P("prompt"),
            P(),
        ),
        out_specs=(wide, resp, resp, prompt, prompt),
        check_vma=False,
    )
```

```python
import functools
import math

import jax
import jax.numpy as jnp
from jax import lax
from jax.experimental import pallas as pl
from jax.experimental.pallas import tpu as pltpu
from jax.sharding import PartitionSpec as P

HEADS = 4
QPK = 8
HD = 128
SHARD = 48
ROWS = HEADS * SHARD
KV = 2 * ROWS
PAY = KV + 16
RING = 8
PAIR = 2
SCALE = HD ** (-0.5)
LOG2E = math.log2(math.e)
DEAD = 1e30
WHOLE = pl.BlockSpec(memory_space=pltpu.VMEM)
GRANT = 20
SMALL = 4
NT = (((1,), (1,)), ((), ()))
NN = (((1,), (0,)), ((), ()))
TN = (((0,), (0,)), ((), ()))
F32, BF16 = jnp.float32, jnp.bfloat16


def dot(a, b, dims):
    return lax.dot_general(a, b, dims, preferred_element_type=F32)


def cost(flops, traffic):
    return pl.CostEstimate(flops=flops, bytes_accessed=traffic, transcendentals=0)


def split_body(live_ref, pk_ref, pv_ref, mine_ref, theirs_ref):
    core, member = lax.axis_index("tensor"), lax.axis_index("group")
    part = pk_ref.shape[1]
    slot = (member * 2 + core) * part + lax.broadcasted_iota(jnp.int32, pk_ref.shape[1:], 0)
    keys = jnp.where(slot < live_ref[0], pk_ref[0].astype(F32), 0.0)
    for at, x in enumerate((keys, pv_ref[0].astype(F32))):
        x = jnp.transpose(x, (1, 0, 2))
        low, high = x[:HEADS], x[HEADS:]
        mine_ref[at] = jnp.where(core == 0, low, high)
        theirs_ref[at] = jnp.where(core == 0, high, low)


def split_heads(live, pk, pv):
    part = pk.shape[1]
    whole = pl.BlockSpec(memory_space=pltpu.VMEM)
    half = jax.ShapeDtypeStruct((2, HEADS, part, HD), F32)
    return pl.pallas_call(
        split_body,
        in_specs=[pl.BlockSpec(memory_space=pltpu.SMEM), whole, whole],
        out_specs=[whole, whole],
        out_shape=[half, half],
        compiler_params=pltpu.CompilerParams(vmem_limit_bytes=SMALL << 20),
        cost_estimate=cost(5 * 10**9, 1 << 20),
        name="split",
    )(live, pk, pv)


def join_body(reward_ref, length_ref, mine_ref, got_ref, out_ref):
    core = lax.axis_index("tensor")
    for at in range(2):
        for h in range(HEADS):
            a, b = mine_ref[at, h], got_ref[at, h]
            pair = [jnp.where(core == 0, a, b), jnp.where(core == 0, b, a)]
            first = (at * HEADS + h) * SHARD
            out_ref[first : first + SHARD] = jnp.concatenate(pair, 0).astype(BF16)
    reward, length = reward_ref[0, 0], length_ref[0, 0]
    line = lax.broadcasted_iota(jnp.int32, (16, HD), 0)
    note = jnp.where(line == 0, reward >> 5, jnp.where(line == 1, reward & 31, length))
    out_ref[KV:] = note.astype(F32).astype(BF16)


def join_tokens(reward, length, mine, got):
    whole = pl.BlockSpec(memory_space=pltpu.VMEM)
    number = pl.BlockSpec(memory_space=pltpu.SMEM)
    return pl.pallas_call(
        join_body,
        in_specs=[number] * 2 + [whole] * 2,
        out_specs=whole,
        out_shape=jax.ShapeDtypeStruct((PAY, HD), BF16),
        compiler_params=pltpu.CompilerParams(vmem_limit_bytes=SMALL << 20),
        cost_estimate=cost(5 * 10**9, 1 << 20),
        name="join",
    )(reward, length, mine, got)


def pair_body(wait_ref, own_ref, beside_ref, out_ref):
    out_ref[:PAY] = own_ref[...]
    out_ref[PAY:] = beside_ref[...]


def join_pair(wait, own, beside):
    return pl.pallas_call(
        pair_body,
        in_specs=[pl.BlockSpec(memory_space=pl.ANY), WHOLE, WHOLE],
        out_specs=WHOLE,
        out_shape=jax.ShapeDtypeStruct((PAIR * PAY, HD), BF16),
        compiler_params=pltpu.CompilerParams(vmem_limit_bytes=SMALL << 20),
        name="pair",
    )(wait, own, beside)


def rows_body(reward_ref, length_ref, task_ref, weights_ref, own_ref, rk_ref, rv_ref, lse_ref, *refs):
    rkt_ref, rvt_ref, row_ref, aux_ref, again_ref = refs
    again_ref[...] = own_ref[...]
    toks = rk_ref.shape[0]
    rows = toks * QPK
    weight = jnp.float32(0.0)
    for kind in range(weights_ref.shape[0]):
        weight = jnp.where(task_ref[0] == kind, weights_ref[kind], weight)
    line = lax.broadcasted_iota(jnp.int32, (8, HD), 0)
    note = jnp.where(line == 0, reward_ref[0, 0], length_ref[0, 0]).astype(F32)
    aux_ref[...] = jnp.where(line < 2, note, weight)
    for src, dst in ((rk_ref, rkt_ref), (rv_ref, rvt_ref)):
        dst[...] = jnp.transpose(src[...].astype(F32), (1, 0, 2)).astype(BF16)
    spread = lax.broadcasted_iota(jnp.int32, (toks, rows), 1) // QPK
    spread = (spread == lax.broadcasted_iota(jnp.int32, (toks, rows), 0)).astype(BF16)
    parts = []
    for h in range(HEADS):
        x = lse_ref[h] * LOG2E
        for _ in range(3):
            parts.append(x.astype(BF16))
            x = x - parts[-1].astype(F32)
    wide = dot(jnp.concatenate(parts, 0), spread, NN)
    line = lax.broadcasted_iota(jnp.int32, (QPK, rows), 0)
    lane = lax.broadcasted_iota(jnp.int32, (QPK, rows), 1)
    for h in range(HEADS):
        at = h * 3 * QPK
        x = wide[at : at + QPK] + (wide[at + QPK : at + 2 * QPK] + wide[at + 2 * QPK : at + 3 * QPK])
        x = jnp.sum(jnp.where(lane % QPK == line, x, 0.0), axis=0, keepdims=True)
        row_ref[h] = jnp.where(lane[0:1] // QPK < length_ref[0, 0], x, DEAD)


def resp_rows(reward, length, task, weights, own, rk, rv, lse):
    toks = rk.shape[0]
    by_head = jax.ShapeDtypeStruct((HEADS, toks, HD), BF16)
    return pl.pallas_call(
        rows_body,
        in_specs=[pl.BlockSpec(memory_space=pltpu.SMEM)] * 4 + [WHOLE] * 4,
        out_specs=[WHOLE] * 5,
        out_shape=[
            by_head,
            by_head,
            jax.ShapeDtypeStruct((HEADS, 1, toks * QPK), F32),
            jax.ShapeDtypeStruct((8, HD), F32),
            jax.ShapeDtypeStruct(own.shape, BF16),
        ],
        compiler_params=pltpu.CompilerParams(vmem_limit_bytes=GRANT << 20),
        cost_estimate=cost(5 * 10**9, 1 << 20),
        name="rows",
    )(reward, length, task, weights, own, rk, rv, lse)


def loop(body):
    lax.fori_loop(0, HEADS, lambda h, c: (body(h), c)[1], 0)


def resp_body(step, q_ref, go_ref, ao_ref, lse_ref, rk_ref, rv_ref, del_ref, ds_ref, dk_ref, dv_ref):
    toks = q_ref.shape[0]
    tb = step // QPK
    ones = jnp.ones((8, HD), BF16)

    def head(h):
        for i in reversed(range(toks // tb)):
            tok = pl.ds(i * tb, tb)
            cols = pl.ds(i * step, step)
            seen = (i + 1) * tb
            q = q_ref[tok, h].reshape(step, HD)
            go = go_ref[tok, h].reshape(step, HD)
            prod = go.astype(F32) * ao_ref[tok, h].reshape(step, HD).astype(F32)
            high = prod.astype(BF16)
            low = (prod - high.astype(F32)).astype(BF16)
            delta = (dot(ones, high, NT) + dot(ones, low, NT))[0:1]
            del_ref[h, :, cols] = delta
            k, v = rk_ref[h, :seen], rv_ref[h, :seen]
            s = dot(k, q, NT) * (SCALE * LOG2E) - lse_ref[h, :, cols]
            p = jnp.exp2(s)
            key = lax.broadcasted_iota(jnp.int32, (tb, step), 0)
            query = lax.broadcasted_iota(jnp.int32, (tb, step), 1) // QPK
            edge = jnp.where(key <= query, p[i * tb :], 0.0)
            p = jnp.concatenate([p[: i * tb], edge], 0) if i else edge
            ds = p * (dot(v, go, NT) - delta)
            pb, dsb = p.astype(BF16), ds.astype(BF16)
            ds_ref[h, :seen, cols] = dsb
            if seen < toks:
                ds_ref[h, seen:, cols] = jnp.zeros((toks - seen, step), BF16)
                dk_ref[h, :seen] += dot(dsb, q, NN)
                dv_ref[h, :seen] += dot(pb, go, NN)
            else:
                dk_ref[h] = dot(dsb, q, NN)
                dv_ref[h] = dot(pb, go, NN)

    loop(head)


def resp_grads(q, go, ao, lse, rk, rv):
    toks = q.shape[0]
    rows = toks * QPK
    return pl.pallas_call(
        functools.partial(resp_body, 1024),
        in_specs=[WHOLE] * 6,
        out_specs=[WHOLE] * 4,
        out_shape=[
            jax.ShapeDtypeStruct((HEADS, 1, rows), F32),
            jax.ShapeDtypeStruct((HEADS, toks, rows), BF16),
            jax.ShapeDtypeStruct((HEADS, toks, HD), F32),
            jax.ShapeDtypeStruct((HEADS, toks, HD), F32),
        ],
        compiler_params=pltpu.CompilerParams(vmem_limit_bytes=GRANT << 20),
        cost_estimate=cost(5 * 10**9, 1 << 20),
        name="resp",
    )(q, go, ao, lse, rk, rv)


def shard_keys(refs, h):
    k, v = [], []
    for r in refs:
        for at in range(0, r.shape[0], PAY):
            k.append(r[pl.ds(pl.multiple_of(at + h * SHARD, 16), SHARD)])
            v.append(r[pl.ds(pl.multiple_of(at + ROWS + h * SHARD, 16), SHARD)])
    return jnp.concatenate(k, 0), jnp.concatenate(v, 0)


def shard_rewards(refs):
    got = []
    for r in refs:
        for at in range(0, r.shape[0], PAY):
            tail = r[pl.ds(at + KV, 16)].astype(F32)
            got.append((tail[0:1] * 32.0 + tail[1:2], tail[2:3]))
    return got


def prompt_body(step, n, waits, notes, last, q_ref, go_ref, lse_ref, del_ref, stat_in, *refs):
    aux = refs[0] if last else None
    refs = refs[1:] if last else refs
    kv, refs = refs[:n], refs[n + waits :]
    ds_ref, outs, stat_ref = refs[0], refs[1:-1], refs[-1]
    toks = q_ref.shape[0]
    tb = step // QPK
    got = shard_rewards(kv)
    total, square = stat_in[0:1], stat_in[1:2]
    for r, _ in got:
        total, square = total + r, square + r * r
    stat_ref[...] = stat_in[...]
    stat_ref[0:1], stat_ref[1:2] = total, square
    for at, which in enumerate(notes):
        stat_ref[2 * at + 2 : 2 * at + 3], stat_ref[2 * at + 3 : 2 * at + 4] = got[which]
    factor = None
    if last:
        members = float(RING * PAIR)
        whole, pairs = total.astype(jnp.int32), square.astype(jnp.int32)
        spare = (RING * PAIR * pairs - whole * whole).astype(F32)
        spread = jnp.sqrt(jnp.maximum(spare, 0.0)) * (1.0 / (members * 256.0))
        weight = aux[2:3] / jnp.maximum(spread, 1.0)
        coefs = []
        for r, length in ((aux[0:1], aux[1:2]), (stat_in[2:3], stat_in[3:4]), (stat_in[4:5], stat_in[5:6])):
            coefs.append((r * members - total) * (1.0 / (members * 256.0)) * weight / length)
        for at, c in enumerate(coefs):
            stat_ref[at : at + 1] = c
        factor = coefs[0]

    def head(h):
        k, v = shard_keys(kv, h)
        dk = dv = None
        for i in range(toks // tb):
            tok = pl.ds(i * tb, tb)
            cols = pl.ds(i * step, step)
            q = q_ref[tok, h].reshape(step, HD)
            go = go_ref[tok, h].reshape(step, HD)
            p = jnp.exp2(dot(k, q, NT) * (SCALE * LOG2E) - lse_ref[h, :, cols])
            ds = p * (dot(v, go, NT) - del_ref[h, :, cols])
            pb, dsb = p.astype(BF16), ds.astype(BF16)
            ds_ref[h, :, cols] = dsb
            a, b = dot(dsb, q, NN), dot(pb, go, NN)
            dk, dv = (a, b) if dk is None else (dk + a, dv + b)
        dk = dk * SCALE
        if last:
            dk, dv = dk * factor, dv * factor
        at = 0
        for out in outs:
            for y in range(out.shape[0]):
                out[y, 0, h] = dk[at : at + SHARD].astype(BF16)
                out[y, 1, h] = dv[at : at + SHARD].astype(BF16)
                at += SHARD

    loop(head)


def prompt_grads(name, q, go, lse, delta, stat, aux, shards, notes, last, *waits):
    rows = q.shape[0] * QPK
    keys = sum(x.shape[0] // PAY for x in shards) * SHARD
    extra = [aux] if last else []
    ins = [q, go, lse, delta, stat, *extra, *shards]
    sizes = [x.shape[0] // PAY for x in shards]
    sums = [jax.ShapeDtypeStruct((n, 2, HEADS, SHARD, HD), BF16) for n in sizes]
    got = pl.pallas_call(
        functools.partial(prompt_body, 1024, len(shards), len(waits), notes, last),
        in_specs=[WHOLE] * len(ins) + [pl.BlockSpec(memory_space=pl.ANY)] * len(waits),
        out_specs=[WHOLE] * (len(sums) + 2),
        out_shape=[
            jax.ShapeDtypeStruct((HEADS, keys, rows), BF16),
            *sums,
            jax.ShapeDtypeStruct((8, HD), F32),
        ],
        compiler_params=pltpu.CompilerParams(vmem_limit_bytes=GRANT << 20),
        cost_estimate=cost((keys // 192) * 5 * 10**9 + 10**8, 1 << 20),
        name=name,
    )(*ins, *waits)
    return got[0], [x.reshape(x.shape[0] * KV, HD) for x in got[1:-1]], got[-1]


def query_body(head, n_ds, counts, ins, coef_ref, *refs):
    ds, shards, rk_ref = refs[:n_ds], refs[n_ds : n_ds + sum(counts)], refs[n_ds + sum(counts)]
    out, coef_out, rows_ref, sems = refs[ins - 1 :]
    step = 512
    tb = step // QPK
    keys, at = [], 0
    for c in counts:
        keys.append(shard_keys(shards[at : at + c], head)[0])
        at += c
    keys.append(rk_ref[head])
    coef_out[...] = coef_ref[...]
    factor = coef_ref[0:1] * SCALE
    sends = []
    for i in range(ds[0].shape[2] // step):
        acc = None
        for d, k in zip(ds, keys):
            a = dot(k, d[head, :, pl.ds(i * step, step)], TN)
            acc = a if acc is None else acc + a
        rows_ref[i * tb : (i + 1) * tb] = (acc.T * factor).astype(BF16).reshape(tb, QPK, HD)
        tok = pl.ds(i * tb, tb)
        sends.append(pltpu.make_async_copy(rows_ref.at[tok], out.at[tok, head], sems.at[i]))
        sends[-1].start()
    for send in sends:
        send.wait()


def query_grads(head, coef, ds, groups, rk, so_far, *waits):
    toks = ds[0].shape[2] // QPK
    counts = [len(g) for g in groups]
    shards = [s for g in groups for s in g]
    there = pl.BlockSpec(memory_space=pl.ANY)
    ins = [coef, *ds, *shards, rk]
    specs = [WHOLE] * len(ins) + [there] * len(waits)
    ins += waits
    alias = {}
    if so_far is not None:
        alias = {len(ins): 0}
        ins.append(so_far)
        specs.append(there)
    return pl.pallas_call(
        functools.partial(query_body, head, len(ds), counts, len(ins)),
        in_specs=specs,
        out_specs=[there, WHOLE],
        out_shape=[
            jax.ShapeDtypeStruct((toks, HEADS, QPK, HD), BF16),
            jax.ShapeDtypeStruct((8, HD), F32),
        ],
        input_output_aliases=alias,
        scratch_shapes=[pltpu.VMEM((toks, QPK, HD), BF16), pltpu.SemaphoreType.DMA((4,))],
        compiler_params=pltpu.CompilerParams(vmem_limit_bytes=GRANT << 20),
        cost_estimate=cost(4 * 10**9, 1 << 20),
        name="dq",
    )(*ins)


def out_body(coef_ref, dk_ref, dv_ref, drk_ref, drv_ref, coef_out):
    coef_out[...] = coef_ref[...]
    factor = coef_ref[0:1]
    for src, dst, c in ((dk_ref, drk_ref, factor * SCALE), (dv_ref, drv_ref, factor)):
        dst[...] = jnp.transpose(src[...] * c, (1, 0, 2)).astype(BF16)


def resp_out(coef, dk, dv):
    out = jax.ShapeDtypeStruct((dk.shape[1], HEADS, HD), BF16)
    return pl.pallas_call(
        out_body,
        in_specs=[WHOLE] * 3,
        out_specs=[WHOLE] * 3,
        out_shape=[out, out, jax.ShapeDtypeStruct((8, HD), F32)],
        compiler_params=pltpu.CompilerParams(vmem_limit_bytes=GRANT << 20),
        cost_estimate=cost(4 * 10**9, 1 << 20),
        name="out",
    )(coef, dk, dv)


def hop(x, dz, dy=0):
    pairs = [
        (z * PAIR + y, ((z + dz) % RING) * PAIR + (y + dy) % PAIR)
        for z in range(RING)
        for y in range(PAIR)
    ]
    return lax.ppermute(x, "group", pairs)


def swap_core(x):
    return lax.ppermute(x, "tensor", [(0, 1), (1, 0)])


def in_order(core, mine, other, axis):
    return jnp.where(
        core == 0,
        jnp.concatenate([mine, other], axis),
        jnp.concatenate([other, mine], axis),
    )


def on_device(
    queries,
    resp_keys,
    resp_values,
    prompt_keys,
    prompt_values,
    attn_out,
    grad_out,
    log_sums,
    prompt_lengths,
    resp_lengths,
    rewards,
    task_ids,
    task_weights,
):

    core = lax.axis_index("tensor")
    member = lax.axis_index("group")
    part = prompt_keys.shape[1]

    mine, theirs = split_heads(prompt_lengths, prompt_keys, prompt_values)
    own = join_tokens(rewards, resp_lengths, mine, swap_core(theirs))

    q, go, ao = queries[0, 0], grad_out[0, 0], attn_out[0, 0]
    rk, rv, lse, aux, again = resp_rows(
        rewards,
        resp_lengths,
        task_ids,
        task_weights,
        own,
        resp_keys[0, 0],
        resp_values[0, 0],
        log_sums[0, 0],
    )
    stat = jnp.zeros((8, HD), F32)

    far = hop(again, 4)
    delta, ds_r, dk_r, dv_r = resp_grads(q, go, ao, lse, rk, rv)
    pair = join_pair(lse, own, hop(own, 0, 1))
    back1, fore1 = hop(pair, 1), hop(pair, -1)
    far_x = hop(far, 0, 1)
    back2, fore2 = hop(back1, 1), hop(fore1, -1)
    back3, fore3 = hop(back2, 1), hop(fore2, -1)

    common = (q, go, lse, delta)
    ds_1, (here, down_1, up_1), stat = prompt_grads(
        "near", *common, stat, None, [pair, back1, fore1], (PAIR, 2 * PAIR), False, far
    )
    ds_2, (down_2, up_2, down_4, up_4), stat = prompt_grads(
        "second", *common, stat, None, [back2, fore2, far, far_x], (), False
    )
    down_4, up_4 = hop(down_4, -1), hop(up_4, 1)
    ds_3, (down_3, up_3), coef = prompt_grads(
        "third", *common, stat, aux, [back3, fore3], (), True
    )

    groups = [[pair, back1, fore1], [back2, fore2, far, far_x], [back3, fore3]]
    ds_all = [ds_1, ds_2, ds_3, ds_r]

    def dq(head, so_far, *waits):
        return query_grads(head, coef, ds_all, groups, rk, so_far, *waits)

    def add(a, c, b):
        return (a.astype(F32) + c[0:1] * b.astype(F32)).astype(BF16)

    down = jnp.concatenate([add(down_3[:KV], coef[2:3], down_4), down_3[KV:]], 0)
    up = jnp.concatenate([up_3[:KV], add(up_3[KV:], coef[1:2], up_4)], 0)
    down, up = hop(down, -1), hop(up, 1)
    grad_q, _ = dq(0, None)
    grad_q, again = dq(1, grad_q)
    down, up = add(down, again, down_2), add(up, again, up_2)
    grad_q, again = dq(2, grad_q, down, up)
    drk, drv, again = resp_out(again, dk_r, dv_r)
    down, up = hop(down, -1), hop(up, 1)
    down, up = add(down, again, down_1), add(up, again, up_1)
    grad_q, again = dq(3, grad_q, down, up)
    down, up = hop(down, -1), hop(up, 1)
    home = again[0:1] * here.astype(F32)
    home = home + down.astype(F32) + up.astype(F32)
    beside = hop(home[KV:].astype(BF16), 0, 1)
    home = (home[:KV] + beside.astype(F32)).reshape(2, HEADS, 2, part, HD)
    keep = lax.dynamic_index_in_dim(home, core, 2, keepdims=False)
    give = lax.dynamic_index_in_dim(home, 1 - core, 2, keepdims=False)
    take = swap_core(give)
    done = in_order(core, keep, take, 1).transpose(0, 2, 1, 3).astype(BF16)
    slot = (member * 2 + core) * part + jnp.arange(part)
    done = jnp.where((slot < prompt_lengths[0])[None, :, None, None], done, 0)
    return (
        grad_q[None, None],
        drk[None, None],
        drv[None, None],
        done[0][None],
        done[1][None],
    )


def solution(mesh):
    wide = P("prompt", "group", None, "tensor", None, None)
    resp = P("prompt", "group", None, "tensor", None)
    prompt = P("prompt", ("group", "tensor"), None, None)
    return jax.shard_map(
        on_device,
        mesh=mesh,
        in_specs=(
            wide,
            resp,
            resp,
            prompt,
            prompt,
            wide,
            wide,
            P("prompt", "group", "tensor", None, None),
            P("prompt"),
            P("prompt", "group"),
            P("prompt", "group"),
            P("prompt"),
            P(),
        ),
        out_specs=(wide, resp, resp, prompt, prompt),
        check_vma=False,
    )
```
